32 devices in a mesh: blk: 4 (over y, x), grp: 8 (over z, core).
Axes of the slice: x: 2, y: 2, z: 4, core: 2. Of those that a mesh axis runs over, the one named last changes fastest.
Arguments:
- batch: bfloat16 [512, 768], P('blk'), may hold values from -6 to 6
- targets: float32 [512, 512], P('blk'), may hold values from -6 to 6
- centers: bfloat16 [32768, 768], P(('blk', 'grp')), may hold values from -6 to 6
- weights: float32 [32768, 512], P(('blk', 'grp')), may hold values from -96 to 96
- eigvec: float32 [2048, 160], P(('blk', 'grp')), may hold values from -0.625 to 0.625
- eig_scale: float32 [160], replicated, may hold values from 0.05 to 0.95
- step: float32 [1], replicated, may hold values from 488.28125 to 1464.8438
Outputs:
- predictions: float32 [512, 512], P('blk')
- new_weights: float32 [32768, 512], P(('blk', 'grp'))
The draws below stay inside these ranges and needn't reach their ends.
All inputs are finite; a program needn't handle non-finite values.
Results may differ from the reference program's by a relative error of at most 0.00075.
Values may be sent and summed in bfloat16 or wider, within the bound.
A program may use at most 64 MiB of HBM per device.

```python
import math
import jax
import jax.numpy as jnp
from jax import lax

D = 768
C = 512
CEN_DEV = 1024
NYS_DEV = 64
Q = 160
CENTERS = 32768
BATCH = 512
NYS = 2048


def shard_levels(rng, extent, shards, least, largest):
    gain = 1.0
    for position, blocks in shards:
        heights = jax.random.uniform(jax.random.fold_in(jax.random.fold_in(rng, 6), position), (blocks,), jnp.float32, least / len(shards), largest / len(shards))
        gain = gain * jnp.repeat(jnp.exp(heights), extent[position] // blocks).reshape((-1,) + (1,) * (len(extent) - 1 - position))
    return gain


def bell_draw(own_key, dims, scale, bound, shards=(), held_as=jnp.bfloat16):
    level = shard_levels(own_key, dims, shards, -0.22, 0.18) if shards else 1.0
    drawn = jax.random.normal(own_key, dims, jnp.float32) * scale * level
    return jnp.minimum(jnp.maximum(drawn, -bound), bound).astype(held_as)


def setup_inputs(seed: int = 0) -> dict:
    keys = jax.random.split(jax.random.key(seed), 8)
    batch = bell_draw(keys[0], (BATCH, D), 1.0, 6.0, ((0, 4),))
    targets = bell_draw(keys[1], (BATCH, C), 1.0, 6.0, ((0, 4),), jnp.float32)
    centers = bell_draw(keys[2], (CENTERS, D), 1.0, 6.0, ((0, 32),))
    weights = bell_draw(keys[3], (CENTERS, C), (2981.0 * CENTERS ** -0.5), 96.0, ((0, 32),), jnp.float32)
    eigvec = bell_draw(keys[4], (NYS, Q), ((NYS * Q) ** -0.25), 0.625, ((0, 32),), jnp.float32)
    eig_scale = jnp.clip(jnp.exp(jax.random.uniform(keys[5], (Q,), jnp.float32, math.log(0.05), math.log(0.95))), 0.05, 0.95)
    step = jnp.clip(jnp.exp(jax.random.uniform(keys[6], (1,), jnp.float32, math.log(488.28125), math.log(1464.8438))), 488.28125, 1464.8438)
    return dict(batch=batch, targets=targets, centers=centers, weights=weights, eigvec=eigvec, eig_scale=eig_scale, step=step)


def kernel_block(cen, rows):
    cen_sq = jnp.sum(cen.astype(jnp.float32) ** 2, axis=1)
    row_sq = jnp.sum(rows.astype(jnp.float32) ** 2, axis=1)
    cross = jnp.dot(cen, rows.T, preferred_element_type=jnp.float32)
    dist = cen_sq[:, None] + row_sq[None, :] - 2.0 * cross
    return jnp.exp(-dist * (4.0 / cen.shape[1]))


def reference(batch, targets, centers, weights, eigvec, eig_scale, step):
    nblocks = centers.shape[0] // CEN_DEV
    cen_blocks = centers.reshape(nblocks, CEN_DEV, centers.shape[1])
    wgt_blocks = weights.reshape(nblocks, CEN_DEV, weights.shape[1])

    def add_block(total, pair):
        kern = kernel_block(pair[0], batch)
        term = lax.dot_general(kern, pair[1], (((0,), (0,)), ((), ())), precision=lax.Precision.HIGHEST, preferred_element_type=jnp.float32)
        return total + term, None

    start = jnp.zeros((batch.shape[0], weights.shape[1]), jnp.float32)
    predictions, unused = lax.scan(add_block, start, (cen_blocks, wgt_blocks))
    residual = predictions - targets

    def grad_block(cen):
        kern = kernel_block(cen, batch)
        return jnp.dot(kern, residual, precision=lax.Precision.HIGHEST, preferred_element_type=jnp.float32)

    grad = lax.map(grad_block, cen_blocks)
    grad_sub = grad[:, :NYS_DEV].reshape(nblocks * NYS_DEV, weights.shape[1])
    proj = jnp.dot(eigvec.T, grad_sub, precision=lax.Precision.HIGHEST, preferred_element_type=jnp.float32)
    corr = jnp.dot(eigvec, eig_scale[:, None] * proj, precision=lax.Precision.HIGHEST, preferred_element_type=jnp.float32)
    corr = corr.reshape(nblocks, NYS_DEV, weights.shape[1])
    precond = jnp.concatenate([grad[:, :NYS_DEV] - corr, grad[:, NYS_DEV:]], axis=1)
    new_weights = weights - step[0] * precond.reshape(weights.shape)
    return predictions, new_weights
```

```python
import jax
import jax.numpy as jnp
from jax import lax
from jax.sharding import PartitionSpec as P

HIGH = lax.Precision.HIGH


def kernel_block(cen, rows):
    cen_sq = jnp.sum(cen.astype(jnp.float32) ** 2, axis=1)
    row_sq = jnp.sum(rows.astype(jnp.float32) ** 2, axis=1)
    cross = jnp.dot(cen, rows.T, preferred_element_type=jnp.float32)
    dist = cen_sq[:, None] + row_sq[None, :] - 2.0 * cross
    return jnp.exp(-dist * (4.0 / cen.shape[1]))


def contract_rows(a, b):
    return lax.dot_general(
        a, b, (((0,), (0,)), ((), ())), precision=HIGH, preferred_element_type=jnp.float32
    )


def local(batch, targets, centers, weights, eigvec, eig_scale, step):
    nys_rows = eigvec.shape[0]
    outs = weights.shape[1]
    rows = lax.all_gather(batch, "blk", axis=0, tiled=True)
    kern = kernel_block(centers, rows)
    part = jnp.concatenate(
        [contract_rows(kern, weights), contract_rows(kern[:nys_rows], eigvec)], axis=1
    )
    part = lax.psum_scatter(part, "blk", scatter_dimension=0, tiled=True)
    part = lax.psum(part, "grp")
    predictions = part[:, :outs]
    residual = predictions - targets
    shared = jnp.concatenate([residual, part[:, outs:]], axis=1).astype(jnp.bfloat16)
    shared = lax.all_gather(shared, "blk", axis=0, tiled=True)
    residual = shared[:, :outs]
    proj = lax.dot_general(
        shared[:, outs:], residual, (((0,), (0,)), ((), ())), preferred_element_type=jnp.float32
    )
    grad = jnp.dot(
        kern, residual.astype(jnp.float32), precision=HIGH, preferred_element_type=jnp.float32
    )
    corr = jnp.dot(
        eigvec, eig_scale[:, None] * proj, precision=HIGH, preferred_element_type=jnp.float32
    )
    precond = jnp.concatenate([grad[:nys_rows] - corr, grad[nys_rows:]], axis=0)
    return (predictions, weights - step[0] * precond)


def solution(mesh):
    return jax.shard_map(
        local,
        mesh=mesh,
        in_specs=(
            P("blk", None),
            P("blk", None),
            P(("blk", "grp"), None),
            P(("blk", "grp"), None),
            P(("blk", "grp"), None),
            P(),
            P(),
        ),
        out_specs=(P("blk", None), P(("blk", "grp"), None)),
        check_vma=False,
    )
```

```python
import functools

import jax
import jax.numpy as jnp
from jax import lax
from jax.experimental import pallas as pl
from jax.experimental.pallas import tpu as pltpu
from jax.sharding import PartitionSpec as P

MESH = pl.DeviceIdType.MESH
F32 = jnp.float32
BF16 = jnp.bfloat16
LANES = 128


def split(v):
    hi = v.astype(BF16)
    return hi, (v - hi.astype(F32)).astype(BF16)


def dot(a, b):
    return jnp.dot(a, b, preferred_element_type=F32)


def dot_nt(a, b):
    return lax.dot_general(a, b, (((1,), (1,)), ((), ())), preferred_element_type=F32)


def kernel(
    n, nz,
    batch, targets, centers, weights, eigvec, eig_t, eig_scale, step,
    pred_out, new_out,
    xall, w_hi, w_lo, csq, ktf, k_hi, k_lo, pall, mall, pc, mc, pb, mb, acc, macc, zb, mz,
    pred, rall, mfull,
    bxs, bxr, fxs, fxr, cps, cpr, cms, cmr, bps, bpr, bms, bmr, zps, zpr, zms, zmr,
    prs, prr, pxs, pxr, grs, grr, gbs, gbr, gms, gmr, frs, frr, fms, fmr,
):
    b0 = lax.axis_index("blk")
    g = lax.axis_index("grp")
    c = lax.rem(g, 2)
    zz = lax.div(g, 2)
    sib = g + 1 - 2 * c
    rows = batch.shape[0]
    half = rows // 2
    q = eig_t.shape[0]
    qh = q // 2
    nys = eigvec.shape[0]
    d = batch.shape[1]
    outs = weights.shape[1]
    ncol = min(nz, outs // LANES)
    cw = outs // ncol
    nrow = nz // ncol
    rz = half // nrow
    mine = pl.ds(pl.multiple_of(c * half, half), half)
    other = pl.ds(pl.multiple_of((1 - c) * half, half), half)
    qmine = pl.ds(pl.multiple_of(c * qh, qh), qh)
    qother = pl.ds(pl.multiple_of((1 - c) * qh, qh), qh)

    def copy(src, dst, ss, rs, to):
        return pltpu.make_async_remote_copy(
            src_ref=src, dst_ref=dst, send_sem=ss, recv_sem=rs, device_id=to, device_id_type=MESH
        )

    def fwd(k):
        return lax.rem(b0 + k, n)

    def back(k):
        return lax.rem(b0 + n - k, n)

    def zdev(z):
        return (b0, z * 2 + c)

    barrier = pltpu.get_barrier_semaphore()
    for k in range(1, n):
        pl.semaphore_signal(barrier, inc=1, device_id=(fwd(k), g), device_id_type=MESH)
    for k in range(1, nz):
        pl.semaphore_signal(barrier, inc=1, device_id=zdev(lax.rem(zz + k, nz)), device_id_type=MESH)
    pl.semaphore_signal(barrier, inc=1, device_id=(b0, sib), device_id_type=MESH)
    pl.semaphore_wait(barrier, n + nz - 1)

    def bx(k):
        return copy(batch.at[mine], xall.at[b0, mine], bxs.at[k], bxr.at[k], (fwd(k), g))

    for k in range(1, n):
        bx(k).start()

    wv = weights[...]
    hi, lo = split(wv)
    w_hi[...] = hi
    w_lo[...] = lo
    cen_sq = jnp.sum(centers[...].astype(F32) ** 2, axis=1, keepdims=True)
    csq[...] = jnp.broadcast_to(cen_sq, (cen_sq.shape[0], rows)).T

    def fx(k):
        p = back(k)
        return copy(xall.at[p, mine], xall.at[p, mine], fxs.at[k], fxr.at[k], (b0, sib))

    def cp(k):
        p = back(k)
        return copy(pall.at[p, other], pc.at[p], cps.at[k], cpr.at[k], (b0, sib))

    def cm(k):
        p = back(k)
        return copy(mall.at[p, qother], mc.at[p], cms.at[k], cmr.at[k], (b0, sib))

    def bp(k):
        p = back(k)
        return copy(pall.at[p, mine], pb.at[b0], bps.at[k], bpr.at[k], (p, g))

    def bm(k):
        p = back(k)
        return copy(mall.at[p, qmine], mb.at[b0], bms.at[k], bmr.at[k], (p, g))

    def chunk(k, x):
        p = back(k)
        x_sq = jnp.sum(x.astype(F32) ** 2, axis=1, keepdims=True)
        dist = csq[...] + x_sq - 2.0 * dot_nt(x, centers[...])
        kt = jnp.exp(-dist * (4.0 / d))
        ktf[p] = kt
        khi, klo = split(kt)
        both = dot(jnp.concatenate([khi, klo], axis=0), w_hi[...])
        pall[p] = both[:rows] + both[rows:] + dot(khi, w_lo[...])
        mall[p] = dot_nt(eig_t[...].astype(BF16), khi[:, :nys]).astype(BF16)
        cp(k).start()
        cm(k).start()

    def core_sum(k):
        p = back(k)
        cp(k).wait()
        cm(k).wait()
        pall[p, mine] = pall[p, mine] + pc[p]
        mall[p, qmine] = (mall[p, qmine].astype(F32) + mc[p].astype(F32)).astype(BF16)

    chunk(0, batch[...])

    def relay(k, carry):
        bx(k).wait()
        fx(k).start()
        return carry

    lax.fori_loop(1, n, relay, 0)

    def work(k, carry):
        fx(k).wait()
        chunk(k, xall[back(k)])

        @pl.when(k >= 2)
        def _():
            core_sum(k - 1)
            bp(k - 1).start()
            bm(k - 1).start()

        return carry

    lax.fori_loop(1, n, work, 0)
    core_sum(n - 1)
    bp(n - 1).start()
    bm(n - 1).start()
    core_sum(0)

    def turn(p, carry):
        th, tl = split(ktf[p].T)
        at = pl.ds(pl.multiple_of(p * rows, rows), rows)
        k_hi[:, at] = th
        k_lo[:, at] = tl
        return carry

    lax.fori_loop(0, n, turn, 0)

    acc[...] = pall[b0, mine]
    macc[...] = mall[b0, qmine].astype(F32)

    def gather_sum(k, carry):
        s = fwd(k)
        bp(k).wait()
        bm(k).wait()
        acc[...] += pb[s]
        macc[...] += mb[s].astype(F32)
        return carry

    lax.fori_loop(1, n, gather_sum, 0)

    def rows_of(z):
        return pl.multiple_of(lax.div(z, ncol) * rz, rz)

    def cols_of(z):
        return pl.ds(pl.multiple_of(lax.rem(z, ncol) * cw, cw), cw)

    def zp(k):
        z = lax.rem(zz + k, nz)
        return copy(
            acc.at[pl.ds(rows_of(z), rz), cols_of(z)], zb.at[zz], zps.at[k], zpr.at[k], zdev(z)
        )

    def zm(k):
        z = lax.rem(zz + k, nz)
        return copy(mz.at[zz], mz.at[zz], zms.at[k], zmr.at[k], zdev(z))

    for k in range(1, nz):
        zp(k).start()
    mz[zz] = macc[...].astype(BF16)
    for k in range(1, nz):
        zm(k).start()
    total = acc[pl.ds(rows_of(zz), rz), cols_of(zz)]
    for k in range(1, nz):
        zp(k).wait()
        total = total + zb[lax.rem(zz + nz - k, nz)]
    my_rows = pl.ds(pl.multiple_of(c * half + rows_of(zz), rz), rz)
    my_cols = cols_of(zz)
    pred[my_rows, my_cols] = total
    rall[b0, my_rows, my_cols] = (total - targets[my_rows, my_cols]).astype(BF16)

    def gr(k):
        at = rall.at[b0, my_rows, my_cols]
        return copy(at, at, grs.at[k], grr.at[k], zdev(lax.rem(zz + k, nz)))

    def pr(k):
        at = pred.at[my_rows, my_cols]
        return copy(at, at, prs.at[k], prr.at[k], zdev(lax.rem(zz + k, nz)))

    for k in range(1, nz):
        gr(k).start()
    for k in range(1, nz):
        pr(k).start()
    msum = mz[zz].astype(F32)
    for k in range(1, nz):
        zm(k).wait()
        msum = msum + mz[lax.rem(zz + nz - k, nz)].astype(F32)
    mfull[b0, qmine] = msum.astype(BF16)

    def gm(k):
        at = mfull.at[b0, qmine]
        return copy(at, at, gms.at[k], gmr.at[k], (fwd(k), g))

    def gb(k):
        at = rall.at[b0, mine]
        return copy(at, at, gbs.at[k], gbr.at[k], (fwd(k), g))

    def fr(k):
        at = rall.at[back(k), mine]
        return copy(at, at, frs.at[k], frr.at[k], (b0, sib))

    def fm(k):
        at = mfull.at[back(k), qmine]
        return copy(at, at, fms.at[k], fmr.at[k], (b0, sib))

    for k in range(1, nz):
        gr(k).wait()
    for k in range(1, n):
        gb(k).start()
    for k in range(1, n):
        gm(k).start()
    fr(0).start()
    fm(0).start()
    for k in range(1, n):
        gb(k).wait()
        fr(k).start()
        gm(k).wait()
        fm(k).start()
    for k in range(1, nz):
        pr(k).wait()
    px = copy(pred.at[mine], pred.at[mine], pxs, pxr, (b0, sib))
    px.start()
    for k in range(n):
        fr(k).wait()
        fm(k).wait()

    res = rall[...].reshape(n * rows, outs)
    rate = step[0]
    tile = 256 if weights.shape[0] % 256 == 0 else nys

    def update(t, carry):
        at = pl.ds(pl.multiple_of(t * tile, tile), tile)
        grad = dot(k_hi[at, :], res) + dot(k_lo[at, :], res)
        new_out[at, :] = weights[at, :] - rate * grad
        return carry

    lax.fori_loop(0, weights.shape[0] // tile, update, 0)
    proj = dot(mfull[0], rall[0])
    for p in range(1, n):
        proj = proj + dot(mfull[p], rall[p])
    corr = jnp.dot(
        eigvec[...], eig_scale[...] * proj, precision=lax.Precision.HIGHEST,
        preferred_element_type=F32,
    )
    new_out[:nys, :] = new_out[:nys, :] + rate * corr
    px.wait()
    pred_out[...] = pred[...]


def local(n, nz, batch, targets, centers, weights, eigvec, eig_scale, step):
    rows, d = batch.shape
    cen, outs = weights.shape
    q = eigvec.shape[1]
    half, qh = rows // 2, q // 2
    ncol = min(nz, outs // LANES)
    rz, cw = half // (nz // ncol), outs // ncol
    vmem = pl.BlockSpec(memory_space=pltpu.VMEM)
    dma = pltpu.SemaphoreType.DMA
    return pl.pallas_call(
        functools.partial(kernel, n, nz),
        out_shape=(
            jax.ShapeDtypeStruct((rows, outs), F32),
            jax.ShapeDtypeStruct((cen, outs), F32),
        ),
        in_specs=[vmem] * 7 + [pl.BlockSpec(memory_space=pltpu.SMEM)],
        out_specs=(vmem, vmem),
        scratch_shapes=[
            pltpu.VMEM((n, rows, d), BF16),
            pltpu.VMEM((cen, outs), BF16),
            pltpu.VMEM((cen, outs), BF16),
            pltpu.VMEM((rows, cen), F32),
            pltpu.VMEM((n, rows, cen), F32),
            pltpu.VMEM((cen, n * rows), BF16),
            pltpu.VMEM((cen, n * rows), BF16),
            pltpu.VMEM((n, rows, outs), F32),
            pltpu.VMEM((n, q, rows), BF16),
            pltpu.VMEM((n, half, outs), F32),
            pltpu.VMEM((n, qh, rows), BF16),
            pltpu.VMEM((n, half, outs), F32),
            pltpu.VMEM((n, qh, rows), BF16),
            pltpu.VMEM((half, outs), F32),
            pltpu.VMEM((qh, rows), F32),
            pltpu.VMEM((nz, rz, cw), F32),
            pltpu.VMEM((nz, qh, rows), BF16),
            pltpu.VMEM((rows, outs), F32),
            pltpu.VMEM((n, rows, outs), BF16),
            pltpu.VMEM((n, q, rows), BF16),
        ]
        + [dma((n,))] * 12
        + [dma((nz,))] * 6
        + [dma(()), dma(())]
        + [dma((nz,))] * 2
        + [dma((n,))] * 8,
        compiler_params=pltpu.CompilerParams(
            collective_id=0, has_side_effects=True, vmem_limit_bytes=48 * 1024 * 1024
        ),
        cost_estimate=pl.CostEstimate(
            flops=10 * cen * n * rows * outs, bytes_accessed=12 * cen * outs,
            transcendentals=cen * n * rows,
        ),
    )(batch, targets, centers, weights, eigvec, eigvec.T, eig_scale[:, None], step)


def solution(mesh):
    n, nz = mesh.shape["blk"], mesh.shape["grp"] // 2
    return jax.shard_map(
        functools.partial(local, n, nz),
        mesh=mesh,
        in_specs=(
            P("blk", None),
            P("blk", None),
            P(("blk", "grp"), None),
            P(("blk", "grp"), None),
            P(("blk", "grp"), None),
            P(),
            P(),
        ),
        out_specs=(P("blk", None), P(("blk", "grp"), None)),
        check_vma=False,
    )
```

```python
import functools

import jax
import jax.numpy as jnp
from jax import lax
from jax.experimental import pallas as pl
from jax.experimental.pallas import tpu as pltpu
from jax.sharding import PartitionSpec as P

MESH = pl.DeviceIdType.MESH
F32 = jnp.float32
BF16 = jnp.bfloat16
LANES = 128


def split(v):
    hi = v.astype(BF16)
    return hi, (v - hi.astype(F32)).astype(BF16)


def dot(a, b):
    return jnp.dot(a, b, preferred_element_type=F32)


def dot_nt(a, b):
    return lax.dot_general(a, b, (((1,), (1,)), ((), ())), preferred_element_type=F32)


def kernel(
    n, nz,
    batch_h, targets_h, centers_h, weights_h, eigvec_h, scale_h, step,
    pred_out, new_out,
    batch, targets, centers, weights, eigvec, eig_scale,
    xall, w_hi, w_lo, csq, ktf, k_hi, k_lo, pall, mall, pc, mc, pb, mb, acc, macc, zb, mz,
    pred, rall, mfull,
    bxs, bxr, fxs, fxr, cps, cpr, cms, cmr, bps, bpr, bms, bmr, zps, zpr, zms, zmr,
    prs, prr, pxs, pxr, grs, grr, gbs, gbr, gms, gmr, frs, frr, fms, fmr, ins, outs_sem,
):
    b0 = lax.axis_index("blk")
    g = lax.axis_index("grp")
    c = lax.rem(g, 2)
    zz = lax.div(g, 2)
    sib = g + 1 - 2 * c
    rows = batch.shape[0]
    half = rows // 2
    q = eigvec.shape[1]
    qh = q // 2
    nys = eigvec.shape[0]
    d = batch.shape[1]
    outs = weights.shape[1]
    ncol = min(nz, outs // LANES)
    cw = outs // ncol
    nrow = nz // ncol
    rz = half // nrow
    mine = pl.ds(pl.multiple_of(c * half, half), half)
    other = pl.ds(pl.multiple_of((1 - c) * half, half), half)
    qmine = pl.ds(pl.multiple_of(c * qh, qh), qh)
    qother = pl.ds(pl.multiple_of((1 - c) * qh, qh), qh)

    def copy(src, dst, ss, rs, to):
        return pltpu.make_async_remote_copy(
            src_ref=src, dst_ref=dst, send_sem=ss, recv_sem=rs, device_id=to, device_id_type=MESH
        )

    def fwd(k):
        peer, bit = 0, 1
        while bit < n:
            peer = peer + lax.rem(lax.div(b0, bit) + lax.div(jnp.int32(k), bit), 2) * bit
            bit *= 2
        return peer

    back = fwd

    def zdev(z):
        return (b0, z * 2 + c)

    loads = [
        pltpu.make_async_copy(src, dst, ins.at[i])
        for i, (src, dst) in enumerate(
            (
                (batch_h, batch),
                (centers_h, centers),
                (weights_h, weights),
                (eigvec_h, eigvec),
                (scale_h, eig_scale),
                (targets_h, targets),
            )
        )
    ]
    for load in loads:
        load.start()

    barrier = pltpu.get_barrier_semaphore()
    for k in range(1, n):
        pl.semaphore_signal(barrier, inc=1, device_id=(fwd(k), g), device_id_type=MESH)
    for k in range(1, nz):
        pl.semaphore_signal(barrier, inc=1, device_id=zdev(lax.rem(zz + k, nz)), device_id_type=MESH)
    pl.semaphore_signal(barrier, inc=1, device_id=(b0, sib), device_id_type=MESH)
    loads[0].wait()
    pl.semaphore_wait(barrier, n + nz - 1)

    def bx(k):
        return copy(batch.at[mine], xall.at[b0, mine], bxs.at[k], bxr.at[k], (fwd(k), g))

    for k in range(1, n):
        bx(k).start()

    for load in loads[1:]:
        load.wait()
    eig_t = eigvec[...].T.astype(BF16)
    wv = weights[...]
    hi, lo = split(wv)
    w_hi[...] = hi
    w_lo[...] = lo
    cen_sq = jnp.sum(centers[...].astype(F32) ** 2, axis=1, keepdims=True)
    csq[...] = jnp.broadcast_to(cen_sq, (cen_sq.shape[0], rows)).T

    def fx(k):
        p = back(k)
        return copy(xall.at[p, mine], xall.at[p, mine], fxs.at[k], fxr.at[k], (b0, sib))

    def cp(k):
        p = back(k)
        return copy(pall.at[p, other], pc.at[p], cps.at[k], cpr.at[k], (b0, sib))

    def cm(k):
        p = back(k)
        return copy(mall.at[p, qother], mc.at[p], cms.at[k], cmr.at[k], (b0, sib))

    def bp(k):
        p = back(k)
        return copy(pall.at[p, mine], pb.at[b0], bps.at[k], bpr.at[k], (p, g))

    def bm(k):
        p = back(k)
        return copy(mall.at[p, qmine], mb.at[b0], bms.at[k], bmr.at[k], (p, g))

    def chunk(k, x):
        p = back(k)
        x_sq = jnp.sum(x.astype(F32) ** 2, axis=1, keepdims=True)
        dist = csq[...] + x_sq - 2.0 * dot_nt(x, centers[...])
        kt = jnp.exp(-dist * (4.0 / d))
        ktf[p] = kt
        khi, klo = split(kt)
        both = dot(jnp.concatenate([khi, klo], axis=0), w_hi[...])
        pall[p] = both[:rows] + both[rows:] + dot(khi, w_lo[...])
        mall[p] = dot_nt(eig_t, khi[:, :nys]).astype(BF16)
        cp(k).start()
        cm(k).start()

    def core_sum(k):
        p = back(k)
        cp(k).wait()
        cm(k).wait()
        pall[p, mine] = pall[p, mine] + pc[p]
        mall[p, qmine] = (mall[p, qmine].astype(F32) + mc[p].astype(F32)).astype(BF16)

    chunk(0, batch[...])

    def relay(k, carry):
        bx(k).wait()
        fx(k).start()
        return carry

    lax.fori_loop(1, n, relay, 0)

    def work(k, carry):
        fx(k).wait()
        chunk(k, xall[back(k)])

        @pl.when(k >= 2)
        def _():
            core_sum(k - 1)
            bp(k - 1).start()
            bm(k - 1).start()

        return carry

    lax.fori_loop(1, n, work, 0)
    core_sum(n - 1)
    bp(n - 1).start()
    bm(n - 1).start()
    core_sum(0)

    def turn(p, carry):
        th, tl = split(ktf[p].T)
        at = pl.ds(pl.multiple_of(p * rows, rows), rows)
        k_hi[:, at] = th
        k_lo[:, at] = tl
        return carry

    lax.fori_loop(0, n, turn, 0)

    acc[...] = pall[b0, mine]
    macc[...] = mall[b0, qmine].astype(F32)

    def gather_sum(k, carry):
        s = fwd(k)
        bp(k).wait()
        bm(k).wait()
        acc[...] += pb[s]
        macc[...] += mb[s].astype(F32)
        return carry

    lax.fori_loop(1, n, gather_sum, 0)

    def rows_of(z):
        return pl.multiple_of(lax.div(z, ncol) * rz, rz)

    def cols_of(z):
        return pl.ds(pl.multiple_of(lax.rem(z, ncol) * cw, cw), cw)

    def zp(k):
        z = lax.rem(zz + k, nz)
        return copy(
            acc.at[pl.ds(rows_of(z), rz), cols_of(z)], zb.at[zz], zps.at[k], zpr.at[k], zdev(z)
        )

    def zm(k):
        z = lax.rem(zz + k, nz)
        return copy(mz.at[zz], mz.at[zz], zms.at[k], zmr.at[k], zdev(z))

    for k in range(1, nz):
        zp(k).start()
    mz[zz] = macc[...].astype(BF16)
    total = acc[pl.ds(rows_of(zz), rz), cols_of(zz)]
    for k in range(1, nz):
        zp(k).wait()
        total = total + zb[lax.rem(zz + nz - k, nz)]
    my_rows = pl.ds(pl.multiple_of(c * half + rows_of(zz), rz), rz)
    my_cols = cols_of(zz)
    pred[my_rows, my_cols] = total
    rall[b0, my_rows, my_cols] = (total - targets[my_rows, my_cols]).astype(BF16)

    def gr(k):
        at = rall.at[b0, my_rows, my_cols]
        return copy(at, at, grs.at[k], grr.at[k], zdev(lax.rem(zz + k, nz)))

    def pr(k):
        at = pred.at[my_rows, my_cols]
        return copy(at, at, prs.at[k], prr.at[k], zdev(lax.rem(zz + k, nz)))

    for k in range(1, nz):
        gr(k).start()
    for k in range(1, nz):
        zm(k).start()

    def gm(k):
        at = mfull.at[b0, qmine]
        return copy(at, at, gms.at[k], gmr.at[k], (fwd(k), g))

    def gb(k):
        at = rall.at[b0, mine]
        return copy(at, at, gbs.at[k], gbr.at[k], (fwd(k), g))

    def fr(k):
        at = rall.at[back(k), mine]
        return copy(at, at, frs.at[k], frr.at[k], (b0, sib))

    def fm(k):
        at = mfull.at[back(k), qmine]
        return copy(at, at, fms.at[k], fmr.at[k], (b0, sib))

    for k in range(1, nz):
        gr(k).wait()
    for k in range(1, n):
        gb(k).start()
    fr(0).start()
    msum = mz[zz].astype(F32)
    for k in range(1, nz):
        zm(k).wait()
        msum = msum + mz[lax.rem(zz + nz - k, nz)].astype(F32)
    mfull[b0, qmine] = msum.astype(BF16)
    for k in range(1, nz):
        pr(k).start()
    for k in range(1, n):
        gb(k).wait()
        fr(k).start()
    for k in range(1, n):
        gm(k).start()
    fm(0).start()
    for k in range(n):
        fr(k).wait()

    res = rall[...].reshape(n * rows, outs)
    rate = step[0]
    tile = 256 if weights.shape[0] % 256 == 0 else nys
    tiles = weights.shape[0] // tile

    def put(t):
        at = pl.ds(pl.multiple_of(t * tile, tile), tile)
        return pltpu.make_async_copy(weights.at[at], new_out.at[at], outs_sem.at[t])

    def update(t):
        at = pl.ds(pl.multiple_of(t * tile, tile), tile)
        grad = dot(k_hi[at, :], res) + dot(k_lo[at, :], res)
        weights[at, :] = weights[at, :] - rate * grad

    def update_out(t, carry):
        update(t)
        put(t).start()
        return carry

    lax.fori_loop(1, tiles, update_out, 0)
    for k in range(1, n):
        gm(k).wait()
        fm(k).start()
    for k in range(1, nz):
        pr(k).wait()
    px = copy(pred.at[mine], pred.at[mine], pxs, pxr, (b0, sib))
    px.start()
    update(jnp.int32(0))
    for k in range(n):
        fm(k).wait()
    proj = dot(mfull[0], rall[0])
    for p in range(1, n):
        proj = proj + dot(mfull[p], rall[p])
    corr = jnp.dot(
        eigvec[...] * eig_scale[...], proj, precision=lax.Precision.HIGHEST,
        preferred_element_type=F32,
    )
    weights[:nys, :] = weights[:nys, :] + rate * corr
    put(jnp.int32(0)).start()
    px.wait()
    put_pred = pltpu.make_async_copy(pred, pred_out, outs_sem.at[tiles])
    put_pred.start()

    def put_wait(t, carry):
        put(t).wait()
        return carry

    lax.fori_loop(0, tiles, put_wait, 0)
    put_pred.wait()


def local(n, nz, batch, targets, centers, weights, eigvec, eig_scale, step):
    rows, d = batch.shape
    cen, outs = weights.shape
    q = eigvec.shape[1]
    half, qh = rows // 2, q // 2
    ncol = min(nz, outs // LANES)
    rz, cw = half // (nz // ncol), outs // ncol
    hbm = pl.BlockSpec(memory_space=pl.ANY)
    tile = 256 if cen % 256 == 0 else eigvec.shape[0]
    dma = pltpu.SemaphoreType.DMA
    return pl.pallas_call(
        functools.partial(kernel, n, nz),
        out_shape=(
            jax.ShapeDtypeStruct((rows, outs), F32),
            jax.ShapeDtypeStruct((cen, outs), F32),
        ),
        in_specs=[hbm] * 6 + [pl.BlockSpec(memory_space=pltpu.SMEM)],
        out_specs=(hbm, hbm),
        scratch_shapes=[
            pltpu.VMEM((rows, d), BF16),
            pltpu.VMEM((rows, outs), F32),
            pltpu.VMEM((cen, d), BF16),
            pltpu.VMEM((cen, outs), F32),
            pltpu.VMEM(eigvec.shape, F32),
            pltpu.VMEM((1, q), F32),
            pltpu.VMEM((n, rows, d), BF16),
            pltpu.VMEM((cen, outs), BF16),
            pltpu.VMEM((cen, outs), BF16),
            pltpu.VMEM((rows, cen), F32),
            pltpu.VMEM((n, rows, cen), F32),
            pltpu.VMEM((cen, n * rows), BF16),
            pltpu.VMEM((cen, n * rows), BF16),
            pltpu.VMEM((n, rows, outs), F32),
            pltpu.VMEM((n, q, rows), BF16),
            pltpu.VMEM((n, half, outs), F32),
            pltpu.VMEM((n, qh, rows), BF16),
            pltpu.VMEM((n, half, outs), F32),
            pltpu.VMEM((n, qh, rows), BF16),
            pltpu.VMEM((half, outs), F32),
            pltpu.VMEM((qh, rows), F32),
            pltpu.VMEM((nz, rz, cw), F32),
            pltpu.VMEM((nz, qh, rows), BF16),
            pltpu.VMEM((rows, outs), F32),
            pltpu.VMEM((n, rows, outs), BF16),
            pltpu.VMEM((n, q, rows), BF16),
        ]
        + [dma((n,))] * 12
        + [dma((nz,))] * 6
        + [dma(()), dma(())]
        + [dma((nz,))] * 2
        + [dma((n,))] * 8
        + [dma((6,)), dma((cen // tile + 1,))],
        compiler_params=pltpu.CompilerParams(
            collective_id=0, has_side_effects=True, vmem_limit_bytes=48 * 1024 * 1024
        ),
        cost_estimate=pl.CostEstimate(
            flops=10 * cen * n * rows * outs, bytes_accessed=12 * cen * outs,
            transcendentals=cen * n * rows,
        ),
    )(batch, targets, centers, weights, eigvec, eig_scale[None, :], step)


def solution(mesh):
    n, nz = mesh.shape["blk"], mesh.shape["grp"] // 2
    return jax.shard_map(
        functools.partial(local, n, nz),
        mesh=mesh,
        in_specs=(
            P("blk", None),
            P("blk", None),
            P(("blk", "grp"), None),
            P(("blk", "grp"), None),
            P(("blk", "grp"), None),
            P(),
            P(),
        ),
        out_specs=(P("blk", None), P(("blk", "grp"), None)),
        check_vma=False,
    )
```

```python
import functools

import jax
import jax.numpy as jnp
from jax import lax
from jax.experimental import pallas as pl
from jax.experimental.pallas import tpu as pltpu
from jax.sharding import PartitionSpec as P

MESH = pl.DeviceIdType.MESH
F32 = jnp.float32
BF16 = jnp.bfloat16
LANES = 128


def split(v):
    hi = v.astype(BF16)
    return hi, (v - hi.astype(F32)).astype(BF16)


def dot(a, b):
    return jnp.dot(a, b, preferred_element_type=F32)


def dot_nt(a, b):
    return lax.dot_general(a, b, (((1,), (1,)), ((), ())), preferred_element_type=F32)


def kernel(
    n, nz,
    batch_h, targets_h, centers_h, weights_h, eigvec_h, scale_h, step,
    pred_out, new_out,
    batch, targets, centers, weights, eigvec, eig_scale,
    xall, w_hi, w_lo, csq, ktf, k_hi, k_lo, pall, mall, pc, mc, pb, mb, acc, macc, zb, mz,
    pred, rall, mfull,
    bxs, bxr, fxs, fxr, cps, cpr, cms, cmr, bps, bpr, bms, bmr, zps, zpr, zms, zmr,
    prs, prr, pxs, pxr, grs, grr, gbs, gbr, gms, gmr, frs, frr, fms, fmr, ins, outs_sem,
):
    b0 = lax.axis_index("blk")
    g = lax.axis_index("grp")
    c = lax.rem(g, 2)
    zz = lax.div(g, 2)
    sib = g + 1 - 2 * c
    rows = batch.shape[0]
    half = rows // 2
    q = eigvec.shape[1]
    qh = q // 2
    nys = eigvec.shape[0]
    d = batch.shape[1]
    outs = weights.shape[1]
    ncol = min(nz, outs // LANES)
    cw = outs // ncol
    nrow = nz // ncol
    rz = half // nrow
    mine = pl.ds(pl.multiple_of(c * half, half), half)
    other = pl.ds(pl.multiple_of((1 - c) * half, half), half)
    qmine = pl.ds(pl.multiple_of(c * qh, qh), qh)
    qother = pl.ds(pl.multiple_of((1 - c) * qh, qh), qh)

    def copy(src, dst, ss, rs, to):
        return pltpu.make_async_remote_copy(
            src_ref=src, dst_ref=dst, send_sem=ss, recv_sem=rs, device_id=to, device_id_type=MESH
        )

    def fwd(k):
        peer, bit = 0, 1
        while bit < n:
            peer = peer + lax.rem(lax.div(b0, bit) + lax.div(jnp.int32(k), bit), 2) * bit
            bit *= 2
        return peer

    back = fwd

    def zdev(z):
        return (b0, z * 2 + c)

    loads = [
        pltpu.make_async_copy(src, dst, ins.at[i])
        for i, (src, dst) in enumerate(
            (
                (batch_h, batch),
                (centers_h, centers),
                (weights_h, weights),
                (eigvec_h, eigvec),
                (scale_h, eig_scale),
                (targets_h, targets),
            )
        )
    ]
    for load in loads:
        load.start()

    barrier = pltpu.get_barrier_semaphore()
    for k in range(1, n):
        pl.semaphore_signal(barrier, inc=1, device_id=(fwd(k), g), device_id_type=MESH)
    for k in range(1, nz):
        pl.semaphore_signal(barrier, inc=1, device_id=zdev(lax.rem(zz + k, nz)), device_id_type=MESH)
    pl.semaphore_signal(barrier, inc=1, device_id=(b0, sib), device_id_type=MESH)
    loads[0].wait()
    pl.semaphore_wait(barrier, n + nz - 1)

    def bx(k):
        return copy(batch.at[mine], xall.at[b0, mine], bxs.at[k], bxr.at[k], (fwd(k), g))

    for k in range(1, n):
        bx(k).start()

    for load in loads[1:]:
        load.wait()
    eig_t = eigvec[...].T.astype(BF16)
    wv = weights[...]
    hi, lo = split(wv)
    w_hi[...] = hi
    w_lo[...] = lo
    cen_sq = jnp.sum(centers[...].astype(F32) ** 2, axis=1, keepdims=True)
    csq[...] = jnp.broadcast_to(cen_sq, (cen_sq.shape[0], rows)).T

    def fx(k):
        p = back(k)
        return copy(xall.at[p, mine], xall.at[p, mine], fxs.at[k], fxr.at[k], (b0, sib))

    def cp(k):
        p = back(k)
        return copy(pall.at[p, other], pc.at[p], cps.at[k], cpr.at[k], (b0, sib))

    def cm(k):
        p = back(k)
        return copy(mall.at[p, qother], mc.at[p], cms.at[k], cmr.at[k], (b0, sib))

    def bp(k):
        p = back(k)
        return copy(pall.at[p, mine], pb.at[b0], bps.at[k], bpr.at[k], (p, g))

    def bm(k):
        p = back(k)
        return copy(mall.at[p, qmine], mb.at[b0], bms.at[k], bmr.at[k], (p, g))

    def chunk(k, x):
        p = back(k)
        x_sq = jnp.sum(x.astype(F32) ** 2, axis=1, keepdims=True)
        dist = csq[...] + x_sq - 2.0 * dot_nt(x, centers[...])
        kt = jnp.exp(-dist * (4.0 / d))
        ktf[p] = kt
        khi, klo = split(kt)
        both = dot(jnp.concatenate([khi, klo], axis=0), w_hi[...])
        pall[p] = both[:rows] + both[rows:] + dot(khi, w_lo[...])
        mall[p] = dot_nt(eig_t, khi[:, :nys]).astype(BF16)
        cp(k).start()
        cm(k).start()

    def core_sum(k):
        p = back(k)
        cp(k).wait()
        cm(k).wait()
        pall[p, mine] = pall[p, mine] + pc[p]
        mall[p, qmine] = (mall[p, qmine].astype(F32) + mc[p].astype(F32)).astype(BF16)

    chunk(0, batch[...])

    def relay(k):
        bx(k).wait()
        fx(k).start()

    for k in range(1, min(3, n)):
        relay(k)

    def work(k, carry):
        fx(k).wait()
        chunk(k, xall[back(k)])

        @pl.when(k + 2 < n)
        def _():
            relay(k + 2)

        @pl.when(k >= 2)
        def _():
            core_sum(k - 1)
            bp(k - 1).start()
            bm(k - 1).start()

        return carry

    lax.fori_loop(1, n, work, 0)
    core_sum(n - 1)
    bp(n - 1).start()
    bm(n - 1).start()
    core_sum(0)

    def turn(p, carry):
        th, tl = split(ktf[p].T)
        at = pl.ds(pl.multiple_of(p * rows, rows), rows)
        k_hi[:, at] = th
        k_lo[:, at] = tl
        return carry

    lax.fori_loop(0, n, turn, 0)

    acc[...] = pall[b0, mine]
    macc[...] = mall[b0, qmine].astype(F32)

    def gather_sum(k, carry):
        s = fwd(k)
        bp(k).wait()
        bm(k).wait()
        acc[...] += pb[s]
        macc[...] += mb[s].astype(F32)
        return carry

    lax.fori_loop(1, n, gather_sum, 0)

    def rows_of(z):
        return pl.multiple_of(lax.div(z, ncol) * rz, rz)

    def cols_of(z):
        return pl.ds(pl.multiple_of(lax.rem(z, ncol) * cw, cw), cw)

    def zp(k):
        z = lax.rem(zz + k, nz)
        return copy(
            acc.at[pl.ds(rows_of(z), rz), cols_of(z)], zb.at[zz], zps.at[k], zpr.at[k], zdev(z)
        )

    def zm(k):
        z = lax.rem(zz + k, nz)
        return copy(mz.at[zz], mz.at[zz], zms.at[k], zmr.at[k], zdev(z))

    for k in range(1, nz):
        zp(k).start()
    mz[zz] = macc[...].astype(BF16)
    total = acc[pl.ds(rows_of(zz), rz), cols_of(zz)]
    for k in range(1, nz):
        zp(k).wait()
        total = total + zb[lax.rem(zz + nz - k, nz)]
    my_rows = pl.ds(pl.multiple_of(c * half + rows_of(zz), rz), rz)
    my_cols = cols_of(zz)
    pred[my_rows, my_cols] = total
    rall[b0, my_rows, my_cols] = (total - targets[my_rows, my_cols]).astype(BF16)

    def gr(k):
        at = rall.at[b0, my_rows, my_cols]
        return copy(at, at, grs.at[k], grr.at[k], zdev(lax.rem(zz + k, nz)))

    def pr(k):
        at = pred.at[my_rows, my_cols]
        return copy(at, at, prs.at[k], prr.at[k], zdev(lax.rem(zz + k, nz)))

    for k in range(1, nz):
        gr(k).start()
    def gm(k):
        at = mfull.at[b0, qmine]
        return copy(at, at, gms.at[k], gmr.at[k], (fwd(k), g))

    def gb(k, j):
        z = lax.rem(zz + nz - j, nz)
        at = rall.at[
            b0, pl.ds(pl.multiple_of(c * half + rows_of(z), rz), rz), cols_of(z)
        ]
        return copy(at, at, gbs.at[j * n + k], gbr.at[j * n + k], (fwd(k), g))

    def gb_send(j, carry):
        gr(j).wait()
        for k in range(1, n):
            gb(k, j).start()
        return carry

    def fr(k):
        at = rall.at[back(k), mine]
        return copy(at, at, frs.at[k], frr.at[k], (b0, sib))

    def fm(k):
        at = mfull.at[back(k), qmine]
        return copy(at, at, fms.at[k], fmr.at[k], (b0, sib))

    for k in range(1, n):
        gb(k, 0).start()
    for k in range(1, nz):
        zm(k).start()
    lax.fori_loop(1, nz, gb_send, 0)
    fr(0).start()
    msum = mz[zz].astype(F32)
    for k in range(1, nz):
        zm(k).wait()
        msum = msum + mz[lax.rem(zz + nz - k, nz)].astype(F32)
    mfull[b0, qmine] = msum.astype(BF16)
    for k in range(1, n):
        gm(k).start()
    fm(0).start()
    for k in range(1, nz):
        pr(k).start()

    def gb_take(k, carry):
        for j in range(nz):
            gb(k, j).wait()
        fr(k).start()
        return carry

    lax.fori_loop(1, n, gb_take, 0)
    for k in range(n):
        fr(k).wait()

    res = rall[...].reshape(n * rows, outs)
    rate = step[0]
    tile = 256 if weights.shape[0] % 256 == 0 else nys
    tiles = weights.shape[0] // tile

    def put(t):
        at = pl.ds(pl.multiple_of(t * tile, tile), tile)
        return pltpu.make_async_copy(weights.at[at], new_out.at[at], outs_sem.at[t])

    def update(t):
        at = pl.ds(pl.multiple_of(t * tile, tile), tile)
        grad = dot(k_hi[at, :], res) + dot(k_lo[at, :], res)
        weights[at, :] = weights[at, :] - rate * grad

    def update_out(t, carry):
        update(t)
        put(t).start()
        return carry

    lax.fori_loop(1, tiles, update_out, 0)
    for k in range(1, n):
        gm(k).wait()
        fm(k).start()
    for k in range(1, nz):
        pr(k).wait()
    px = copy(pred.at[mine], pred.at[mine], pxs, pxr, (b0, sib))
    px.start()
    update(jnp.int32(0))
    for k in range(n):
        fm(k).wait()
    proj = dot(mfull[0], rall[0])
    for p in range(1, n):
        proj = proj + dot(mfull[p], rall[p])
    corr = jnp.dot(
        eigvec[...] * eig_scale[...], proj, precision=lax.Precision.HIGHEST,
        preferred_element_type=F32,
    )
    weights[:nys, :] = weights[:nys, :] + rate * corr
    put(jnp.int32(0)).start()
    px.wait()
    put_pred = pltpu.make_async_copy(pred, pred_out, outs_sem.at[tiles])
    put_pred.start()

    def put_wait(t, carry):
        put(t).wait()
        return carry

    lax.fori_loop(0, tiles, put_wait, 0)
    put_pred.wait()


def local(n, nz, batch, targets, centers, weights, eigvec, eig_scale, step):
    rows, d = batch.shape
    cen, outs = weights.shape
    q = eigvec.shape[1]
    half, qh = rows // 2, q // 2
    ncol = min(nz, outs // LANES)
    rz, cw = half // (nz // ncol), outs // ncol
    hbm = pl.BlockSpec(memory_space=pltpu.HBM)
    tile = 256 if cen % 256 == 0 else eigvec.shape[0]
    dma = pltpu.SemaphoreType.DMA
    return pl.pallas_call(
        functools.partial(kernel, n, nz),
        out_shape=(
            jax.ShapeDtypeStruct((rows, outs), F32),
            jax.ShapeDtypeStruct((cen, outs), F32),
        ),
        in_specs=[hbm] * 6 + [pl.BlockSpec(memory_space=pltpu.SMEM)],
        out_specs=(hbm, hbm),
        scratch_shapes=[
            pltpu.VMEM((rows, d), BF16),
            pltpu.VMEM((rows, outs), F32),
            pltpu.VMEM((cen, d), BF16),
            pltpu.VMEM((cen, outs), F32),
            pltpu.VMEM(eigvec.shape, F32),
            pltpu.VMEM((1, q), F32),
            pltpu.VMEM((n, rows, d), BF16),
            pltpu.VMEM((cen, outs), BF16),
            pltpu.VMEM((cen, outs), BF16),
            pltpu.VMEM((rows, cen), F32),
            pltpu.VMEM((n, rows, cen), F32),
            pltpu.VMEM((cen, n * rows), BF16),
            pltpu.VMEM((cen, n * rows), BF16),
            pltpu.VMEM((n, rows, outs), F32),
            pltpu.VMEM((n, q, rows), BF16),
            pltpu.VMEM((n, half, outs), F32),
            pltpu.VMEM((n, qh, rows), BF16),
            pltpu.VMEM((n, half, outs), F32),
            pltpu.VMEM((n, qh, rows), BF16),
            pltpu.VMEM((half, outs), F32),
            pltpu.VMEM((qh, rows), F32),
            pltpu.VMEM((nz, rz, cw), F32),
            pltpu.VMEM((nz, qh, rows), BF16),
            pltpu.VMEM((rows, outs), F32),
            pltpu.VMEM((n, rows, outs), BF16),
            pltpu.VMEM((n, q, rows), BF16),
        ]
        + [dma((n,))] * 12
        + [dma((nz,))] * 6
        + [dma(()), dma(())]
        + [dma((nz,))] * 2
        + [dma((n * nz,))] * 2
        + [dma((n,))] * 6
        + [dma((6,)), dma((cen // tile + 1,))],
        compiler_params=pltpu.CompilerParams(
            collective_id=0, has_side_effects=True, vmem_limit_bytes=60 * 1024 * 1024
        ),
        cost_estimate=pl.CostEstimate(
            flops=10 * cen * n * rows * outs, bytes_accessed=12 * cen * outs,
            transcendentals=cen * n * rows,
        ),
    )(batch, targets, centers, weights, eigvec, eig_scale[None, :], step)


def solution(mesh):
    n, nz = mesh.shape["blk"], mesh.shape["grp"] // 2
    return jax.shard_map(
        functools.partial(local, n, nz),
        mesh=mesh,
        in_specs=(
            P("blk", None),
            P("blk", None),
            P(("blk", "grp"), None),
            P(("blk", "grp"), None),
            P(("blk", "grp"), None),
            P(),
            P(),
        ),
        out_specs=(P("blk", None), P(("blk", "grp"), None)),
        check_vma=False,
    )
```

```python
import functools

import jax
import jax.numpy as jnp
from jax import lax
from jax.experimental import pallas as pl
from jax.experimental.pallas import tpu as pltpu
from jax.sharding import PartitionSpec as P

MESH = pl.DeviceIdType.MESH
F32 = jnp.float32
BF16 = jnp.bfloat16
LANES = 128


def split(v):
    hi = v.astype(BF16)
    return hi, (v - hi.astype(F32)).astype(BF16)


def dot(a, b):
    return jnp.dot(a, b, preferred_element_type=F32)


def dot_nt(a, b):
    return lax.dot_general(a, b, (((1,), (1,)), ((), ())), preferred_element_type=F32)


def kernel(
    n, nz,
    batch_h, targets_h, centers_h, weights_h, eigvec_h, scale_h, step,
    pred_out, new_out,
    batch, targets, centers, weights, eigvec, eig_scale,
    xall, w_hi, w_lo, csq, ktf, k_hi, k_lo, pall, mall, pc, mc, pb, mb, acc, macc, zb, mz,
    pred, rall, mfull,
    bxs, bxr, fxs, fxr, cps, cpr, cms, cmr, bps, bpr, bms, bmr, zps, zpr, zms, zmr,
    prs, prr, pxs, pxr, grs, grr, gbs, gbr, gms, gmr, frs, frr, fms, fmr, ins, outs_sem,
):
    b0 = lax.axis_index("blk")
    g = lax.axis_index("grp")
    c = lax.rem(g, 2)
    zz = lax.div(g, 2)
    sib = g + 1 - 2 * c
    rows = batch.shape[0]
    half = rows // 2
    q = eigvec.shape[1]
    qh = q // 2
    nys = eigvec.shape[0]
    d = batch.shape[1]
    outs = weights.shape[1]
    ncol = min(nz, outs // LANES)
    cw = outs // ncol
    nrow = nz // ncol
    rz = half // nrow
    mine = pl.ds(pl.multiple_of(c * half, half), half)
    other = pl.ds(pl.multiple_of((1 - c) * half, half), half)
    qmine = pl.ds(pl.multiple_of(c * qh, qh), qh)
    qother = pl.ds(pl.multiple_of((1 - c) * qh, qh), qh)

    def copy(src, dst, ss, rs, to):
        return pltpu.make_async_remote_copy(
            src_ref=src, dst_ref=dst, send_sem=ss, recv_sem=rs, device_id=to, device_id_type=MESH
        )

    def fwd(k):
        peer, bit = 0, 1
        while bit < n:
            peer = peer + lax.rem(lax.div(b0, bit) + lax.div(jnp.int32(k), bit), 2) * bit
            bit *= 2
        return peer

    back = fwd

    def zdev(z):
        return (b0, z * 2 + c)

    loads = [
        pltpu.make_async_copy(src, dst, ins.at[i])
        for i, (src, dst) in enumerate(
            (
                (batch_h, batch),
                (centers_h, centers),
                (weights_h, weights),
                (eigvec_h, eigvec),
                (scale_h, eig_scale),
                (targets_h, targets),
            )
        )
    ]
    for load in loads:
        load.start()

    barrier = pltpu.get_barrier_semaphore()
    for k in range(1, n):
        pl.semaphore_signal(barrier, inc=1, device_id=(fwd(k), g), device_id_type=MESH)
    for k in range(1, nz):
        pl.semaphore_signal(barrier, inc=1, device_id=zdev(lax.rem(zz + k, nz)), device_id_type=MESH)
    pl.semaphore_signal(barrier, inc=1, device_id=(b0, sib), device_id_type=MESH)
    loads[0].wait()
    pl.semaphore_wait(barrier, n + nz - 1)

    def bx(k):
        return copy(batch.at[mine], xall.at[b0, mine], bxs.at[k], bxr.at[k], (fwd(k), g))

    for k in range(1, n):
        bx(k).start()

    for load in loads[1:]:
        load.wait()
    eig_t = eigvec[...].T.astype(BF16)
    wv = weights[...]
    hi, lo = split(wv)
    w_hi[...] = hi
    w_lo[...] = lo
    cen_sq = jnp.sum(centers[...].astype(F32) ** 2, axis=1, keepdims=True)
    csq[...] = jnp.broadcast_to(cen_sq, (cen_sq.shape[0], rows)).T

    def fx(k):
        p = back(k)
        return copy(xall.at[p, mine], xall.at[p, mine], fxs.at[k], fxr.at[k], (b0, sib))

    def cp(k):
        p = back(k)
        return copy(pall.at[p, other], pc.at[p], cps.at[k], cpr.at[k], (b0, sib))

    def cm(k):
        p = back(k)
        return copy(mall.at[p, qother], mc.at[p], cms.at[k], cmr.at[k], (b0, sib))

    def bp(k):
        p = back(k)
        return copy(pall.at[p, mine], pb.at[b0], bps.at[k], bpr.at[k], (p, g))

    def bm(k):
        p = back(k)
        return copy(mall.at[p, qmine], mb.at[b0], bms.at[k], bmr.at[k], (p, g))

    def chunk(k, x):
        p = back(k)
        x_sq = jnp.sum(x.astype(F32) ** 2, axis=1, keepdims=True)
        dist = csq[...] + x_sq - 2.0 * dot_nt(x, centers[...])
        kt = jnp.exp(-dist * (4.0 / d))
        ktf[p] = kt
        khi, klo = split(kt)
        both = dot(jnp.concatenate([khi, klo], axis=0), w_hi[...])
        pall[p] = both[:rows] + both[rows:] + dot(khi, w_lo[...])
        mall[p] = dot_nt(eig_t, khi[:, :nys]).astype(BF16)
        cp(k).start()
        cm(k).start()

    def core_sum(k):
        p = back(k)
        cp(k).wait()
        cm(k).wait()
        pall[p, mine] = pall[p, mine] + pc[p]
        mall[p, qmine] = (mall[p, qmine].astype(F32) + mc[p].astype(F32)).astype(BF16)

    chunk(0, batch[...])

    def relay(k):
        bx(k).wait()
        fx(k).start()

    for k in range(1, min(3, n)):
        relay(k)

    def work(k, carry):
        fx(k).wait()
        chunk(k, xall[back(k)])

        @pl.when(k + 2 < n)
        def _():
            relay(k + 2)

        @pl.when(k >= 2)
        def _():
            core_sum(k - 1)
            bp(k - 1).start()
            bm(k - 1).start()

        return carry

    lax.fori_loop(1, n, work, 0)
    core_sum(n - 1)
    bp(n - 1).start()
    bm(n - 1).start()
    core_sum(0)

    def turn(p, carry):
        th, tl = split(ktf[p].T)
        at = pl.ds(pl.multiple_of(p * rows, rows), rows)
        k_hi[:, at] = th
        k_lo[:, at] = tl
        return carry

    lax.fori_loop(0, n, turn, 0)

    acc[...] = pall[b0, mine]
    macc[...] = mall[b0, qmine].astype(F32)

    def gather_sum(k, carry):
        s = fwd(k)
        bp(k).wait()
        bm(k).wait()
        acc[...] += pb[s]
        macc[...] += mb[s].astype(F32)
        return carry

    lax.fori_loop(1, n, gather_sum, 0)

    def rows_of(z):
        return pl.multiple_of(lax.div(z, ncol) * rz, rz)

    def cols_of(z):
        return pl.ds(pl.multiple_of(lax.rem(z, ncol) * cw, cw), cw)

    def zp(k):
        z = lax.rem(zz + k, nz)
        return copy(
            acc.at[pl.ds(rows_of(z), rz), cols_of(z)], zb.at[zz], zps.at[k], zpr.at[k], zdev(z)
        )

    def zm(k):
        z = lax.rem(zz + k, nz)
        return copy(mz.at[zz], mz.at[zz], zms.at[k], zmr.at[k], zdev(z))

    for k in range(1, nz):
        zp(k).start()
    mz[zz] = macc[...].astype(BF16)
    total = acc[pl.ds(rows_of(zz), rz), cols_of(zz)]
    for k in range(1, nz):
        zp(k).wait()
        total = total + zb[lax.rem(zz + nz - k, nz)]
    my_rows = pl.ds(pl.multiple_of(c * half + rows_of(zz), rz), rz)
    my_cols = cols_of(zz)
    pred[my_rows, my_cols] = total
    rall[b0, my_rows, my_cols] = (total - targets[my_rows, my_cols]).astype(BF16)

    def gr(k):
        at = rall.at[b0, my_rows, my_cols]
        return copy(at, at, grs.at[k], grr.at[k], zdev(lax.rem(zz + k, nz)))

    def pr(k):
        at = pred.at[my_rows, my_cols]
        return copy(at, at, prs.at[k], prr.at[k], zdev(lax.rem(zz + k, nz)))

    for k in range(1, nz):
        gr(k).start()
    def gm(k):
        at = mfull.at[b0, qmine]
        return copy(at, at, gms.at[k], gmr.at[k], (fwd(k), g))

    def gb(k, j):
        z = lax.rem(zz + nz - j, nz)
        at = rall.at[
            b0, pl.ds(pl.multiple_of(c * half + rows_of(z), rz), rz), cols_of(z)
        ]
        return copy(at, at, gbs.at[j * n + k], gbr.at[j * n + k], (fwd(k), g))

    def gb_send(j, carry):
        gr(j).wait()
        for k in range(1, n):
            gb(k, j).start()
        return carry

    def fr(k):
        at = rall.at[back(k), mine]
        return copy(at, at, frs.at[k], frr.at[k], (b0, sib))

    def fm(k):
        at = mfull.at[back(k), qmine]
        return copy(at, at, fms.at[k], fmr.at[k], (b0, sib))

    for k in range(1, n):
        gb(k, 0).start()
    for k in range(1, nz):
        zm(k).start()
    lax.fori_loop(1, nz, gb_send, 0)
    fr(0).start()
    msum = mz[zz].astype(F32)
    for k in range(1, nz):
        zm(k).wait()
        msum = msum + mz[lax.rem(zz + nz - k, nz)].astype(F32)
    mfull[b0, qmine] = msum.astype(BF16)
    for k in range(1, n):
        gm(k).start()
    fm(0).start()
    for k in range(1, nz):
        pr(k).start()

    def gb_take(k, carry):
        for j in range(nz):
            gb(k, j).wait()
        fr(k).start()
        return carry

    lax.fori_loop(1, n, gb_take, 0)
    for k in range(n):
        fr(k).wait()

    res = rall[...].reshape(n * rows, outs)
    rate = step[0]
    tile = 256 if weights.shape[0] % 256 == 0 else nys
    tiles = weights.shape[0] // tile

    def put(t):
        at = pl.ds(pl.multiple_of(t * tile, tile), tile)
        return pltpu.make_async_copy(weights.at[at], new_out.at[at], outs_sem.at[t])

    def update(t):
        at = pl.ds(pl.multiple_of(t * tile, tile), tile)
        grad = dot(k_hi[at, :], res) + dot(k_lo[at, :], res)
        weights[at, :] = weights[at, :] - rate * grad

    def update_out(t, carry):
        update(t)
        put(t).start()
        return carry

    lax.fori_loop(1, tiles, update_out, 0)
    for k in range(1, n):
        gm(k).wait()
        fm(k).start()
    for k in range(1, nz):
        pr(k).wait()
    px = copy(pred.at[mine], pred.at[mine], pxs, pxr, (b0, sib))
    px.start()
    update(jnp.int32(0))
    for k in range(n):
        fm(k).wait()
    proj = dot(mfull[0], rall[0])
    for p in range(1, n):
        proj = proj + dot(mfull[p], rall[p])
    corr = jnp.dot(
        eigvec[...] * eig_scale[...], proj, precision=lax.Precision.HIGHEST,
        preferred_element_type=F32,
    )
    weights[:nys, :] = weights[:nys, :] + rate * corr
    put(jnp.int32(0)).start()
    px.wait()
    put_pred = pltpu.make_async_copy(pred, pred_out, outs_sem.at[tiles])
    put_pred.start()

    def put_wait(t, carry):
        put(t).wait()
        return carry

    lax.fori_loop(0, tiles, put_wait, 0)
    put_pred.wait()


def local(n, nz, batch, targets, centers, weights, eigvec, eig_scale, step):
    rows, d = batch.shape
    cen, outs = weights.shape
    q = eigvec.shape[1]
    half, qh = rows // 2, q // 2
    ncol = min(nz, outs // LANES)
    rz, cw = half // (nz // ncol), outs // ncol
    hbm = pl.BlockSpec(memory_space=pltpu.HBM)
    tile = 256 if cen % 256 == 0 else eigvec.shape[0]
    dma = pltpu.SemaphoreType.DMA
    pred, new = pl.pallas_call(
        functools.partial(kernel, n, nz),
        out_shape=[
            jax.ShapeDtypeStruct((rows, outs), F32),
            jax.ShapeDtypeStruct((cen, outs), F32),
        ],
        in_specs=[hbm] * 6 + [pl.BlockSpec(memory_space=pltpu.SMEM)],
        out_specs=[pl.BlockSpec(memory_space=pl.ANY)] * 2,
        scratch_shapes=[
            pltpu.VMEM((rows, d), BF16),
            pltpu.VMEM((rows, outs), F32),
            pltpu.VMEM((cen, d), BF16),
            pltpu.VMEM((cen, outs), F32),
            pltpu.VMEM(eigvec.shape, F32),
            pltpu.VMEM((1, q), F32),
            pltpu.VMEM((n, rows, d), BF16),
            pltpu.VMEM((cen, outs), BF16),
            pltpu.VMEM((cen, outs), BF16),
            pltpu.VMEM((rows, cen), F32),
            pltpu.VMEM((n, rows, cen), F32),
            pltpu.VMEM((cen, n * rows), BF16),
            pltpu.VMEM((cen, n * rows), BF16),
            pltpu.VMEM((n, rows, outs), F32),
            pltpu.VMEM((n, q, rows), BF16),
            pltpu.VMEM((n, half, outs), F32),
            pltpu.VMEM((n, qh, rows), BF16),
            pltpu.VMEM((n, half, outs), F32),
            pltpu.VMEM((n, qh, rows), BF16),
            pltpu.VMEM((half, outs), F32),
            pltpu.VMEM((qh, rows), F32),
            pltpu.VMEM((nz, rz, cw), F32),
            pltpu.VMEM((nz, qh, rows), BF16),
            pltpu.VMEM((rows, outs), F32),
            pltpu.VMEM((n, rows, outs), BF16),
            pltpu.VMEM((n, q, rows), BF16),
        ]
        + [dma((n,))] * 12
        + [dma((nz,))] * 6
        + [dma(()), dma(())]
        + [dma((nz,))] * 2
        + [dma((n * nz,))] * 2
        + [dma((n,))] * 6
        + [dma((6,)), dma((cen // tile + 1,))],
        compiler_params=pltpu.CompilerParams(
            collective_id=0, has_side_effects=True, vmem_limit_bytes=48 * 1024 * 1024
        ),
        cost_estimate=pl.CostEstimate(
            flops=10 * cen * n * rows * outs, bytes_accessed=12 * cen * outs,
            transcendentals=cen * n * rows,
        ),
    )(batch, targets, centers, weights, eigvec, eig_scale[None, :], step)
    return pred, new


def solution(mesh):
    n, nz = mesh.shape["blk"], mesh.shape["grp"] // 2
    return jax.shard_map(
        functools.partial(local, n, nz),
        mesh=mesh,
        in_specs=(
            P("blk", None),
            P("blk", None),
            P(("blk", "grp"), None),
            P(("blk", "grp"), None),
            P(("blk", "grp"), None),
            P(),
            P(),
        ),
        out_specs=(P("blk", None), P(("blk", "grp"), None)),
        check_vma=False,
    )
```

```python
import functools

import jax
import jax.numpy as jnp
from jax import lax
from jax.experimental import pallas as pl
from jax.experimental.pallas import tpu as pltpu
from jax.sharding import PartitionSpec as P

MESH = pl.DeviceIdType.MESH
F32 = jnp.float32
BF16 = jnp.bfloat16
LANES = 128


def split(v):
    hi = v.astype(BF16)
    return hi, (v - hi.astype(F32)).astype(BF16)


def dot(a, b):
    return jnp.dot(a, b, preferred_element_type=F32)


def dot_nt(a, b):
    return lax.dot_general(a, b, (((1,), (1,)), ((), ())), preferred_element_type=F32)


def kernel(
    n, nz,
    batch_h, targets_h, centers_h, weights_h, eigvec_h, scale_h, step,
    pred_out, new_out,
    batch, targets, centers, weights, eigvec, eig_scale,
    xall, w_hi, w_lo, csq, ktf, k_hi, k_lo, pall, mall, pc, mc, pb, mb, acc, macc, zb, mz,
    pred, rall, mfull,
    bxs, bxr, fxs, fxr, cps, cpr, cms, cmr, bps, bpr, bms, bmr, zps, zpr, zms, zmr,
    prs, prr, pxs, pxr, grs, grr, gbs, gbr, gms, gmr, frs, frr, fms, fmr, ins, outs_sem,
):
    b0 = lax.axis_index("blk")
    g = lax.axis_index("grp")
    c = lax.rem(g, 2)
    zz = lax.div(g, 2)
    sib = g + 1 - 2 * c
    rows = batch.shape[0]
    half = rows // 2
    q = eigvec.shape[1]
    qh = q // 2
    nys = eigvec.shape[0]
    d = batch.shape[1]
    outs = weights.shape[1]
    ncol = min(nz, outs // LANES)
    cw = outs // ncol
    nrow = nz // ncol
    rz = half // nrow
    mine = pl.ds(pl.multiple_of(c * half, half), half)
    other = pl.ds(pl.multiple_of((1 - c) * half, half), half)
    qmine = pl.ds(pl.multiple_of(c * qh, qh), qh)
    qother = pl.ds(pl.multiple_of((1 - c) * qh, qh), qh)

    def copy(src, dst, ss, rs, to):
        return pltpu.make_async_remote_copy(
            src_ref=src, dst_ref=dst, send_sem=ss, recv_sem=rs, device_id=to, device_id_type=MESH
        )

    def fwd(k):
        peer, bit = 0, 1
        while bit < n:
            peer = peer + lax.rem(lax.div(b0, bit) + lax.div(jnp.int32(k), bit), 2) * bit
            bit *= 2
        return peer

    back = fwd

    def zdev(z):
        return (b0, z * 2 + c)

    loads = [
        pltpu.make_async_copy(src, dst, ins.at[i])
        for i, (src, dst) in enumerate(
            (
                (batch_h, batch),
                (centers_h, centers),
                (weights_h, weights),
                (eigvec_h, eigvec),
                (scale_h, eig_scale),
                (targets_h, targets),
            )
        )
    ]
    for load in loads:
        load.start()

    def rows_of(z):
        return pl.multiple_of(lax.div(z, ncol) * rz, rz)

    def cols_of(z):
        return pl.ds(pl.multiple_of(lax.rem(z, ncol) * cw, cw), cw)

    barrier = pltpu.get_barrier_semaphore()
    for k in range(1, n):
        pl.semaphore_signal(barrier, inc=1, device_id=(fwd(k), g), device_id_type=MESH)
    for k in range(1, nz):
        pl.semaphore_signal(barrier, inc=1, device_id=zdev(lax.rem(zz + k, nz)), device_id_type=MESH)
    pl.semaphore_signal(barrier, inc=1, device_id=(b0, sib), device_id_type=MESH)
    loads[0].wait()
    pl.semaphore_wait(barrier, n + nz - 1)

    def bx(k):
        return copy(batch.at[mine], xall.at[b0, mine], bxs.at[k], bxr.at[k], (fwd(k), g))

    for k in range(1, n):
        bx(k).start()

    for load in loads[1:]:
        load.wait()
    eig_t = eigvec[...].T.astype(BF16)
    wv = weights[...]
    hi, lo = split(wv)
    w_hi[...] = hi
    w_lo[...] = lo
    cen_sq = jnp.sum(centers[...].astype(F32) ** 2, axis=1, keepdims=True)
    csq[...] = jnp.broadcast_to(cen_sq, (cen_sq.shape[0], rows)).T

    def fx(k):
        p = back(k)
        return copy(xall.at[p, mine], xall.at[p, mine], fxs.at[k], fxr.at[k], (b0, sib))

    def cp(k):
        p = back(k)
        return copy(pall.at[p, other], pc.at[p], cps.at[k], cpr.at[k], (b0, sib))

    def cm(k):
        p = back(k)
        return copy(mall.at[p, qother], mc.at[p], cms.at[k], cmr.at[k], (b0, sib))

    def bp(k, j):
        p, z = back(k), lax.rem(zz + j, nz)
        at = pl.ds(pl.multiple_of(c * half + rows_of(z), rz), rz)
        return copy(
            pall.at[p, at, cols_of(z)],
            pb.at[b0, pl.ds(rows_of(z), rz), cols_of(z)],
            bps.at[j * n + k], bpr.at[j * n + k], (p, g),
        )

    def bp_send(k):
        for j in list(range(1, nz)) + [0]:
            bp(k, j).start()
        bm(k).start()

    def bm(k):
        p = back(k)
        return copy(mall.at[p, qmine], mb.at[b0], bms.at[k], bmr.at[k], (p, g))

    def chunk(k, x):
        p = back(k)
        x_sq = jnp.sum(x.astype(F32) ** 2, axis=1, keepdims=True)
        dist = csq[...] + x_sq - 2.0 * dot_nt(x, centers[...])
        kt = jnp.exp(-dist * (4.0 / d))
        ktf[p] = kt
        khi, klo = split(kt)
        both = dot(jnp.concatenate([khi, klo], axis=0), w_hi[...])
        pall[p] = both[:rows] + both[rows:] + dot(khi, w_lo[...])
        mall[p] = dot_nt(eig_t, khi[:, :nys]).astype(BF16)
        cp(k).start()
        cm(k).start()

    def core_sum(k):
        p = back(k)
        cp(k).wait()
        cm(k).wait()
        pall[p, mine] = pall[p, mine] + pc[p]
        mall[p, qmine] = (mall[p, qmine].astype(F32) + mc[p].astype(F32)).astype(BF16)

    chunk(0, batch[...])

    def relay(k):
        bx(k).wait()
        fx(k).start()

    for k in range(1, min(3, n)):
        relay(k)

    def work(k, carry):
        fx(k).wait()
        chunk(k, xall[back(k)])

        @pl.when(k + 2 < n)
        def _():
            relay(k + 2)

        @pl.when(k >= 2)
        def _():
            core_sum(k - 1)
            bp_send(k - 1)

        return carry

    lax.fori_loop(1, n, work, 0)
    core_sum(n - 1)
    bp_send(n - 1)
    core_sum(0)

    def turn(p, carry):
        th, tl = split(ktf[p].T)
        at = pl.ds(pl.multiple_of(p * rows, rows), rows)
        k_hi[:, at] = th
        k_lo[:, at] = tl
        return carry

    lax.fori_loop(0, n // 2, turn, 0)

    def zp(k):
        z = lax.rem(zz + k, nz)
        return copy(
            acc.at[pl.ds(rows_of(z), rz), cols_of(z)], zb.at[zz], zps.at[k], zpr.at[k], zdev(z)
        )

    def zm(k):
        z = lax.rem(zz + k, nz)
        return copy(mz.at[zz], mz.at[zz], zms.at[k], zmr.at[k], zdev(z))

    def piece_sum(j):
        z = lax.rem(zz + j, nz)
        at = pl.ds(pl.multiple_of(c * half + rows_of(z), rz), rz)
        total = pall[b0, at, cols_of(z)]
        for k in range(1, n):
            bp(k, j).wait()
            total = total + pb[fwd(k), pl.ds(rows_of(z), rz), cols_of(z)]
        return total

    def piece_send(j, carry):
        z = lax.rem(zz + j, nz)
        acc[pl.ds(rows_of(z), rz), cols_of(z)] = piece_sum(j)
        zp(j).start()
        return carry

    lax.fori_loop(1, nz, piece_send, 0)
    total = piece_sum(0)
    macc[...] = mall[b0, qmine].astype(F32)
    for k in range(1, n):
        bm(k).wait()
        macc[...] += mb[fwd(k)].astype(F32)
    mz[zz] = macc[...].astype(BF16)
    lax.fori_loop(n // 2, n, turn, 0)
    for k in range(1, nz):
        zp(k).wait()
        total = total + zb[lax.rem(zz + nz - k, nz)]
    my_rows = pl.ds(pl.multiple_of(c * half + rows_of(zz), rz), rz)
    my_cols = cols_of(zz)
    pred[my_rows, my_cols] = total
    rall[b0, my_rows, my_cols] = (total - targets[my_rows, my_cols]).astype(BF16)

    def gr(k):
        at = rall.at[b0, my_rows, my_cols]
        return copy(at, at, grs.at[k], grr.at[k], zdev(lax.rem(zz + k, nz)))

    def pr(k):
        at = pred.at[my_rows, my_cols]
        return copy(at, at, prs.at[k], prr.at[k], zdev(lax.rem(zz + k, nz)))

    for k in range(1, nz):
        gr(k).start()
    def gm(k):
        at = mfull.at[b0, qmine]
        return copy(at, at, gms.at[k], gmr.at[k], (fwd(k), g))

    def gb(k, j):
        z = lax.rem(zz + nz - j, nz)
        at = rall.at[
            b0, pl.ds(pl.multiple_of(c * half + rows_of(z), rz), rz), cols_of(z)
        ]
        return copy(at, at, gbs.at[j * n + k], gbr.at[j * n + k], (fwd(k), g))

    def gb_send(j, carry):
        gr(j).wait()
        for k in range(1, n):
            gb(k, j).start()
        return carry

    def fr(k):
        at = rall.at[back(k), mine]
        return copy(at, at, frs.at[k], frr.at[k], (b0, sib))

    def fm(k):
        at = mfull.at[back(k), qmine]
        return copy(at, at, fms.at[k], fmr.at[k], (b0, sib))

    for k in range(1, n):
        gb(k, 0).start()
    for k in range(1, nz):
        zm(k).start()
    lax.fori_loop(1, nz, gb_send, 0)
    fr(0).start()
    msum = mz[zz].astype(F32)
    for k in range(1, nz):
        zm(k).wait()
        msum = msum + mz[lax.rem(zz + nz - k, nz)].astype(F32)
    mfull[b0, qmine] = msum.astype(BF16)
    for k in range(1, n):
        gm(k).start()
    fm(0).start()
    for k in range(1, nz):
        pr(k).start()

    def gb_take(k, carry):
        for j in range(nz):
            gb(k, j).wait()
        fr(k).start()
        return carry

    lax.fori_loop(1, n, gb_take, 0)
    for k in range(n):
        fr(k).wait()

    res = rall[...].reshape(n * rows, outs)
    rate = step[0]
    tile = 256 if weights.shape[0] % 256 == 0 else nys
    tiles = weights.shape[0] // tile

    def put(t):
        at = pl.ds(pl.multiple_of(t * tile, tile), tile)
        return pltpu.make_async_copy(weights.at[at], new_out.at[at], outs_sem.at[t])

    def update(t):
        at = pl.ds(pl.multiple_of(t * tile, tile), tile)
        grad = dot(k_hi[at, :], res) + dot(k_lo[at, :], res)
        weights[at, :] = weights[at, :] - rate * grad

    def update_out(t, carry):
        update(t)
        put(t).start()
        return carry

    lax.fori_loop(1, tiles, update_out, 0)
    for k in range(1, n):
        gm(k).wait()
        fm(k).start()
    for k in range(1, nz):
        pr(k).wait()
    px = copy(pred.at[mine], pred.at[mine], pxs, pxr, (b0, sib))
    px.start()
    update(jnp.int32(0))
    for k in range(n):
        fm(k).wait()
    proj = dot(mfull[0], rall[0])
    for p in range(1, n):
        proj = proj + dot(mfull[p], rall[p])
    corr = jnp.dot(
        eigvec[...] * eig_scale[...], proj, precision=lax.Precision.HIGHEST,
        preferred_element_type=F32,
    )
    weights[:nys, :] = weights[:nys, :] + rate * corr
    put(jnp.int32(0)).start()
    px.wait()
    put_pred = pltpu.make_async_copy(pred, pred_out, outs_sem.at[tiles])
    put_pred.start()

    def put_wait(t, carry):
        put(t).wait()
        return carry

    lax.fori_loop(0, tiles, put_wait, 0)
    put_pred.wait()


def local(n, nz, batch, targets, centers, weights, eigvec, eig_scale, step):
    rows, d = batch.shape
    cen, outs = weights.shape
    q = eigvec.shape[1]
    half, qh = rows // 2, q // 2
    ncol = min(nz, outs // LANES)
    rz, cw = half // (nz // ncol), outs // ncol
    hbm = pl.BlockSpec(memory_space=pltpu.HBM)
    tile = 256 if cen % 256 == 0 else eigvec.shape[0]
    dma = pltpu.SemaphoreType.DMA
    return pl.pallas_call(
        functools.partial(kernel, n, nz),
        out_shape=(
            jax.ShapeDtypeStruct((rows, outs), F32),
            jax.ShapeDtypeStruct((cen, outs), F32),
        ),
        in_specs=[hbm] * 6 + [pl.BlockSpec(memory_space=pltpu.SMEM)],
        out_specs=(pl.BlockSpec(memory_space=pl.ANY),) * 2,
        scratch_shapes=[
            pltpu.VMEM((rows, d), BF16),
            pltpu.VMEM((rows, outs), F32),
            pltpu.VMEM((cen, d), BF16),
            pltpu.VMEM((cen, outs), F32),
            pltpu.VMEM(eigvec.shape, F32),
            pltpu.VMEM((1, q), F32),
            pltpu.VMEM((n, rows, d), BF16),
            pltpu.VMEM((cen, outs), BF16),
            pltpu.VMEM((cen, outs), BF16),
            pltpu.VMEM((rows, cen), F32),
            pltpu.VMEM((n, rows, cen), F32),
            pltpu.VMEM((cen, n * rows), BF16),
            pltpu.VMEM((cen, n * rows), BF16),
            pltpu.VMEM((n, rows, outs), F32),
            pltpu.VMEM((n, q, rows), BF16),
            pltpu.VMEM((n, half, outs), F32),
            pltpu.VMEM((n, qh, rows), BF16),
            pltpu.VMEM((n, half, outs), F32),
            pltpu.VMEM((n, qh, rows), BF16),
            pltpu.VMEM((half, outs), F32),
            pltpu.VMEM((qh, rows), F32),
            pltpu.VMEM((nz, rz, cw), F32),
            pltpu.VMEM((nz, qh, rows), BF16),
            pltpu.VMEM((rows, outs), F32),
            pltpu.VMEM((n, rows, outs), BF16),
            pltpu.VMEM((n, q, rows), BF16),
        ]
        + [dma((n,))] * 8
        + [dma((n * nz,))] * 2
        + [dma((n,))] * 2
        + [dma((nz,))] * 6
        + [dma(()), dma(())]
        + [dma((nz,))] * 2
        + [dma((n * nz,))] * 2
        + [dma((n,))] * 6
        + [dma((6,)), dma((cen // tile + 1,))],
        compiler_params=pltpu.CompilerParams(
            collective_id=0, has_side_effects=True, vmem_limit_bytes=48 * 1024 * 1024
        ),
        cost_estimate=pl.CostEstimate(
            flops=10 * cen * n * rows * outs, bytes_accessed=12 * cen * outs,
            transcendentals=cen * n * rows,
        ),
    )(
        *(
            pltpu.with_memory_space_constraint(v, pltpu.HBM)
            for v in (batch, targets, centers, weights, eigvec, eig_scale[None, :])
        ),
        step,
    )


def solution(mesh):
    n, nz = mesh.shape["blk"], mesh.shape["grp"] // 2
    return jax.shard_map(
        functools.partial(local, n, nz),
        mesh=mesh,
        in_specs=(
            P("blk", None),
            P("blk", None),
            P(("blk", "grp"), None),
            P(("blk", "grp"), None),
            P(("blk", "grp"), None),
            P(),
            P(),
        ),
        out_specs=(P("blk", None), P(("blk", "grp"), None)),
        check_vma=False,
    )
```

```python
import functools

import jax
import jax.numpy as jnp
from jax import lax
from jax.experimental import pallas as pl
from jax.experimental.pallas import tpu as pltpu
from jax.sharding import PartitionSpec as P

MESH = pl.DeviceIdType.MESH
F32 = jnp.float32
BF16 = jnp.bfloat16
LANES = 128


def split(v):
    hi = v.astype(BF16)
    return hi, (v - hi.astype(F32)).astype(BF16)


def dot(a, b):
    return jnp.dot(a, b, preferred_element_type=F32)


def dot_nt(a, b):
    return lax.dot_general(a, b, (((1,), (1,)), ((), ())), preferred_element_type=F32)


def kernel(
    n, nz,
    batch_h, targets_h, centers_h, weights_h, eigvec_h, scale_h, step,
    pred_out, new_out,
    batch, targets, centers, weights, eigvec, eig_scale,
    xall, w_hi, w_lo, csq, ktf, k_both, pall, mall, pc, mc, pb, mb, acc, macc, zb, mz,
    pred, rall, mfull,
    bxs, bxr, fxs, fxr, cps, cpr, cms, cmr, bps, bpr, bms, bmr, zps, zpr, zms, zmr,
    prs, prr, pxs, pxr, grs, grr, gbs, gbr, gms, gmr, frs, frr, fms, fmr, ins,
):
    b0 = lax.axis_index("blk")
    g = lax.axis_index("grp")
    c = lax.rem(g, 2)
    zz = lax.div(g, 2)
    sib = g + 1 - 2 * c
    rows = batch.shape[0]
    half = rows // 2
    q = eigvec.shape[1]
    qh = q // 2
    nys = eigvec.shape[0]
    d = batch.shape[1]
    outs = weights.shape[1]
    ncol = min(nz, outs // LANES)
    cw = outs // ncol
    nrow = nz // ncol
    rz = half // nrow
    mine = pl.ds(pl.multiple_of(c * half, half), half)
    other = pl.ds(pl.multiple_of((1 - c) * half, half), half)
    qmine = pl.ds(pl.multiple_of(c * qh, qh), qh)
    qother = pl.ds(pl.multiple_of((1 - c) * qh, qh), qh)

    def copy(src, dst, ss, rs, to):
        return pltpu.make_async_remote_copy(
            src_ref=src, dst_ref=dst, send_sem=ss, recv_sem=rs, device_id=to, device_id_type=MESH
        )

    def fwd(k):
        peer, bit = 0, 1
        while bit < n:
            peer = peer + lax.rem(lax.div(b0, bit) + lax.div(jnp.int32(k), bit), 2) * bit
            bit *= 2
        return peer

    back = fwd

    def zdev(z):
        return (b0, z * 2 + c)

    loads = [
        pltpu.make_async_copy(src, dst, ins.at[i])
        for i, (src, dst) in enumerate(
            (
                (batch_h, batch),
                (centers_h, centers),
                (weights_h, weights),
                (eigvec_h, eigvec),
                (scale_h, eig_scale),
                (targets_h, targets),
            )
        )
    ]
    for load in loads:
        load.start()

    def rows_of(z):
        return pl.multiple_of(lax.div(z, ncol) * rz, rz)

    def cols_of(z):
        return pl.ds(pl.multiple_of(lax.rem(z, ncol) * cw, cw), cw)

    barrier = pltpu.get_barrier_semaphore()
    for k in range(1, n):
        pl.semaphore_signal(barrier, inc=1, device_id=(fwd(k), g), device_id_type=MESH)
    for k in range(1, nz):
        pl.semaphore_signal(barrier, inc=1, device_id=zdev(lax.rem(zz + k, nz)), device_id_type=MESH)
    pl.semaphore_signal(barrier, inc=1, device_id=(b0, sib), device_id_type=MESH)
    loads[0].wait()
    pl.semaphore_wait(barrier, n + nz - 1)

    def bx(k):
        return copy(batch.at[mine], xall.at[b0, mine], bxs.at[k], bxr.at[k], (fwd(k), g))

    for k in range(1, n):
        bx(k).start()

    for load in loads[1:]:
        load.wait()
    eig_t = eigvec[...].T.astype(BF16)
    wv = weights[...]
    hi, lo = split(wv)
    w_hi[...] = hi
    w_lo[...] = lo
    cen_sq = jnp.sum(centers[...].astype(F32) ** 2, axis=1, keepdims=True)
    csq[...] = jnp.broadcast_to(cen_sq, (cen_sq.shape[0], rows)).T

    def fx(k):
        p = back(k)
        return copy(xall.at[p, mine], xall.at[p, mine], fxs.at[k], fxr.at[k], (b0, sib))

    def cp(k):
        p = back(k)
        return copy(pall.at[p, other], pc.at[p], cps.at[k], cpr.at[k], (b0, sib))

    def cm(k):
        p = back(k)
        return copy(mall.at[p, qother], mc.at[p], cms.at[k], cmr.at[k], (b0, sib))

    def bp(k, j):
        p, z = back(k), lax.rem(zz + j, nz)
        at = pl.ds(pl.multiple_of(c * half + rows_of(z), rz), rz)
        return copy(
            pall.at[p, at, cols_of(z)],
            pb.at[b0, pl.ds(rows_of(z), rz), cols_of(z)],
            bps.at[j * n + k], bpr.at[j * n + k], (p, g),
        )

    def bp_send(k):
        for j in list(range(1, nz)) + [0]:
            bp(k, j).start()
        bm(k).start()

    def bm(k):
        p = back(k)
        return copy(mall.at[p, qmine], mb.at[b0], bms.at[k], bmr.at[k], (p, g))

    def chunk(k, x):
        p = back(k)
        x_sq = jnp.sum(x.astype(F32) ** 2, axis=1, keepdims=True)
        dist = csq[...] + x_sq - 2.0 * dot_nt(x, centers[...])
        kt = jnp.exp(-dist * (4.0 / d))
        ktf[p] = kt
        khi, klo = split(kt)
        both = dot(jnp.concatenate([khi, klo], axis=0), w_hi[...])
        pall[p] = both[:rows] + both[rows:] + dot(khi, w_lo[...])
        mall[p] = dot_nt(eig_t, khi[:, :nys]).astype(BF16)
        cp(k).start()
        cm(k).start()

    def core_sum(k):
        p = back(k)
        cp(k).wait()
        cm(k).wait()
        pall[p, mine] = pall[p, mine] + pc[p]
        mall[p, qmine] = (mall[p, qmine].astype(F32) + mc[p].astype(F32)).astype(BF16)

    chunk(0, batch[...])

    def relay(k):
        bx(k).wait()
        fx(k).start()

    for k in range(1, min(3, n)):
        relay(k)

    def work(k, carry):
        fx(k).wait()
        chunk(k, xall[back(k)])

        @pl.when(k + 2 < n)
        def _():
            relay(k + 2)

        @pl.when(k >= 2)
        def _():
            core_sum(k - 1)
            bp_send(k - 1)

        return carry

    lax.fori_loop(1, n, work, 0)
    core_sum(n - 1)
    bp_send(n - 1)
    core_sum(0)

    def turn(p, carry):
        th, tl = split(ktf[p].T)
        k_both[p, :, :rows] = th
        k_both[p, :, rows:] = tl
        return carry

    lax.fori_loop(0, n // 2, turn, 0)

    def zp(k):
        z = lax.rem(zz + k, nz)
        return copy(
            acc.at[pl.ds(rows_of(z), rz), cols_of(z)], zb.at[zz], zps.at[k], zpr.at[k], zdev(z)
        )

    def zm(k):
        z = lax.rem(zz + k, nz)
        return copy(mz.at[zz], mz.at[zz], zms.at[k], zmr.at[k], zdev(z))

    def piece_sum(j):
        z = lax.rem(zz + j, nz)
        at = pl.ds(pl.multiple_of(c * half + rows_of(z), rz), rz)
        total = pall[b0, at, cols_of(z)]
        for k in range(1, n):
            bp(k, j).wait()
            total = total + pb[fwd(k), pl.ds(rows_of(z), rz), cols_of(z)]
        return total

    def piece_send(j, carry):
        z = lax.rem(zz + j, nz)
        acc[pl.ds(rows_of(z), rz), cols_of(z)] = piece_sum(j)
        zp(j).start()
        return carry

    lax.fori_loop(1, nz, piece_send, 0)
    total = piece_sum(0)
    macc[...] = mall[b0, qmine].astype(F32)
    for k in range(1, n):
        bm(k).wait()
        macc[...] += mb[fwd(k)].astype(F32)
    mz[zz] = macc[...].astype(BF16)
    lax.fori_loop(n // 2, n, turn, 0)
    for k in range(1, nz):
        zp(k).wait()
        total = total + zb[lax.rem(zz + nz - k, nz)]
    my_rows = pl.ds(pl.multiple_of(c * half + rows_of(zz), rz), rz)
    my_cols = cols_of(zz)
    pred[my_rows, my_cols] = total
    rall[b0, my_rows, my_cols] = (total - targets[my_rows, my_cols]).astype(BF16)

    def gr(k):
        at = rall.at[b0, my_rows, my_cols]
        return copy(at, at, grs.at[k], grr.at[k], zdev(lax.rem(zz + k, nz)))

    def pr(k):
        at = pred.at[my_rows, my_cols]
        return copy(at, at, prs.at[k], prr.at[k], zdev(lax.rem(zz + k, nz)))

    for k in range(1, nz):
        gr(k).start()
    def gm(k):
        at = mfull.at[b0, qmine]
        return copy(at, at, gms.at[k], gmr.at[k], (fwd(k), g))

    def gb(k, j):
        z = lax.rem(zz + nz - j, nz)
        at = rall.at[
            b0, pl.ds(pl.multiple_of(c * half + rows_of(z), rz), rz), cols_of(z)
        ]
        return copy(at, at, gbs.at[j * n + k], gbr.at[j * n + k], (fwd(k), g))

    def gb_send(j, carry):
        gr(j).wait()
        for k in range(1, n):
            gb(k, j).start()
        return carry

    def fr(k):
        at = rall.at[back(k), mine]
        return copy(at, at, frs.at[k], frr.at[k], (b0, sib))

    def fm(k):
        at = mfull.at[back(k), qmine]
        return copy(at, at, fms.at[k], fmr.at[k], (b0, sib))

    for k in range(1, n):
        gb(k, 0).start()
    for k in range(1, nz):
        zm(k).start()
    lax.fori_loop(1, nz, gb_send, 0)
    fr(0).start()
    msum = mz[zz].astype(F32)
    for k in range(1, nz):
        zm(k).wait()
        msum = msum + mz[lax.rem(zz + nz - k, nz)].astype(F32)
    mfull[b0, qmine] = msum.astype(BF16)
    for k in range(1, n):
        gm(k).start()
    fm(0).start()
    for k in range(1, nz):
        pr(k).start()

    rate = step[0]
    tile = 256 if weights.shape[0] % 256 == 0 else nys
    tiles = weights.shape[0] // tile

    def gb_take(k):
        for j in range(nz):
            gb(k, j).wait()
        fr(k).start()

    def update(k, base):
        p = back(k)
        res = jnp.concatenate([rall[p], rall[p]], axis=0)

        def one(t, carry):
            at = pl.ds(pl.multiple_of(t * tile, tile), tile)
            new_out[at, :] = base[at, :] - rate * dot(k_both[p, at, :], res)
            return carry

        lax.fori_loop(0, tiles, one, 0)

    fr(0).wait()
    update(0, weights)
    for k in range(1, min(3, n)):
        gb_take(k)

    def add_chunk(k, carry):
        fr(k).wait()
        update(k, new_out)

        @pl.when(k + 2 < n)
        def _():
            gb_take(k + 2)

        gm(k).wait()
        fm(k).start()
        return carry

    lax.fori_loop(1, n, add_chunk, 0)
    for k in range(1, nz):
        pr(k).wait()
    px = copy(pred.at[mine], pred.at[mine], pxs, pxr, (b0, sib))
    px.start()
    for k in range(n):
        fm(k).wait()
    proj = dot(mfull[0], rall[0])
    for p in range(1, n):
        proj = proj + dot(mfull[p], rall[p])
    corr = jnp.dot(
        eigvec[...] * eig_scale[...], proj, precision=lax.Precision.HIGHEST,
        preferred_element_type=F32,
    )
    new_out[:nys, :] = new_out[:nys, :] + rate * corr
    px.wait()
    pred_out[...] = pred[...]


def local(n, nz, batch, targets, centers, weights, eigvec, eig_scale, step):
    rows, d = batch.shape
    cen, outs = weights.shape
    q = eigvec.shape[1]
    half, qh = rows // 2, q // 2
    ncol = min(nz, outs // LANES)
    rz, cw = half // (nz // ncol), outs // ncol
    hbm = pl.BlockSpec(memory_space=pltpu.HBM)
    dma = pltpu.SemaphoreType.DMA
    return pl.pallas_call(
        functools.partial(kernel, n, nz),
        out_shape=(
            jax.ShapeDtypeStruct((rows, outs), F32),
            jax.ShapeDtypeStruct((cen, outs), F32),
        ),
        in_specs=[hbm] * 6 + [pl.BlockSpec(memory_space=pltpu.SMEM)],
        out_specs=(pl.BlockSpec(memory_space=pltpu.VMEM),) * 2,
        scratch_shapes=[
            pltpu.VMEM((rows, d), BF16),
            pltpu.VMEM((rows, outs), F32),
            pltpu.VMEM((cen, d), BF16),
            pltpu.VMEM((cen, outs), F32),
            pltpu.VMEM(eigvec.shape, F32),
            pltpu.VMEM((1, q), F32),
            pltpu.VMEM((n, rows, d), BF16),
            pltpu.VMEM((cen, outs), BF16),
            pltpu.VMEM((cen, outs), BF16),
            pltpu.VMEM((rows, cen), F32),
            pltpu.VMEM((n, rows, cen), F32),
            pltpu.VMEM((n, cen, 2 * rows), BF16),
            pltpu.VMEM((n, rows, outs), F32),
            pltpu.VMEM((n, q, rows), BF16),
            pltpu.VMEM((n, half, outs), F32),
            pltpu.VMEM((n, qh, rows), BF16),
            pltpu.VMEM((n, half, outs), F32),
            pltpu.VMEM((n, qh, rows), BF16),
            pltpu.VMEM((half, outs), F32),
            pltpu.VMEM((qh, rows), F32),
            pltpu.VMEM((nz, rz, cw), F32),
            pltpu.VMEM((nz, qh, rows), BF16),
            pltpu.VMEM((rows, outs), F32),
            pltpu.VMEM((n, rows, outs), BF16),
            pltpu.VMEM((n, q, rows), BF16),
        ]
        + [dma((n,))] * 8
        + [dma((n * nz,))] * 2
        + [dma((n,))] * 2
        + [dma((nz,))] * 6
        + [dma(()), dma(())]
        + [dma((nz,))] * 2
        + [dma((n * nz,))] * 2
        + [dma((n,))] * 6
        + [dma((6,))],
        compiler_params=pltpu.CompilerParams(
            collective_id=0, has_side_effects=True, vmem_limit_bytes=48 * 1024 * 1024
        ),
        cost_estimate=pl.CostEstimate(
            flops=10 * cen * n * rows * outs, bytes_accessed=12 * cen * outs,
            transcendentals=cen * n * rows,
        ),
    )(
        *(
            pltpu.with_memory_space_constraint(v, pltpu.HBM)
            for v in (batch, targets, centers, weights, eigvec, eig_scale[None, :])
        ),
        step,
    )


def solution(mesh):
    n, nz = mesh.shape["blk"], mesh.shape["grp"] // 2
    return jax.shard_map(
        functools.partial(local, n, nz),
        mesh=mesh,
        in_specs=(
            P("blk", None),
            P("blk", None),
            P(("blk", "grp"), None),
            P(("blk", "grp"), None),
            P(("blk", "grp"), None),
            P(),
            P(),
        ),
        out_specs=(P("blk", None), P(("blk", "grp"), None)),
        check_vma=False,
    )
```

```python
import functools

import jax
import jax.numpy as jnp
from jax import lax
from jax.experimental import pallas as pl
from jax.experimental.pallas import tpu as pltpu
from jax.sharding import PartitionSpec as P

MESH = pl.DeviceIdType.MESH
F32 = jnp.float32
BF16 = jnp.bfloat16
LANES = 128


def split(v):
    hi = v.astype(BF16)
    return hi, (v - hi.astype(F32)).astype(BF16)


def dot(a, b):
    return jnp.dot(a, b, preferred_element_type=F32)


def dot_nt(a, b):
    return lax.dot_general(a, b, (((1,), (1,)), ((), ())), preferred_element_type=F32)


def kernel(
    n, nz,
    batch_h, targets_h, centers_h, weights_h, eigvec_h, scale_h, step,
    pred_out, new_out,
    batch, targets, centers, weights, eigvec, eig_scale,
    xall, w_hi, w_lo, csq, ktf, k_hi, k_lo, pall, mall, pc, mc, pb, mb, acc, macc, zb, mz,
    pred, rall, mfull,
    bxs, bxr, fxs, fxr, cps, cpr, cms, cmr, bps, bpr, bms, bmr, zps, zpr, zms, zmr,
    prs, prr, pxs, pxr, grs, grr, gbs, gbr, gms, gmr, frs, frr, fms, fmr, ins,
):
    b0 = lax.axis_index("blk")
    g = lax.axis_index("grp")
    c = lax.rem(g, 2)
    zz = lax.div(g, 2)
    sib = g + 1 - 2 * c
    rows = batch.shape[0]
    half = rows // 2
    q = eigvec.shape[1]
    qh = q // 2
    nys = eigvec.shape[0]
    d = batch.shape[1]
    outs = weights.shape[1]
    ncol = min(nz, outs // LANES)
    cw = outs // ncol
    nrow = nz // ncol
    rz = half // nrow
    mine = pl.ds(pl.multiple_of(c * half, half), half)
    other = pl.ds(pl.multiple_of((1 - c) * half, half), half)
    qmine = pl.ds(pl.multiple_of(c * qh, qh), qh)
    qother = pl.ds(pl.multiple_of((1 - c) * qh, qh), qh)

    def copy(src, dst, ss, rs, to):
        return pltpu.make_async_remote_copy(
            src_ref=src, dst_ref=dst, send_sem=ss, recv_sem=rs, device_id=to, device_id_type=MESH
        )

    def fwd(k):
        peer, bit = 0, 1
        while bit < n:
            peer = peer + lax.rem(lax.div(b0, bit) + lax.div(jnp.int32(k), bit), 2) * bit
            bit *= 2
        return peer

    back = fwd

    def zdev(z):
        return (b0, z * 2 + c)

    loads = [
        pltpu.make_async_copy(src, dst, ins.at[i])
        for i, (src, dst) in enumerate(
            (
                (batch_h, batch),
                (centers_h, centers),
                (weights_h, weights),
                (eigvec_h, eigvec),
                (scale_h, eig_scale),
                (targets_h, targets),
            )
        )
    ]
    for load in loads:
        load.start()

    def rows_of(z):
        return pl.multiple_of(lax.div(z, ncol) * rz, rz)

    def cols_of(z):
        return pl.ds(pl.multiple_of(lax.rem(z, ncol) * cw, cw), cw)

    barrier = pltpu.get_barrier_semaphore()
    for k in range(1, n):
        pl.semaphore_signal(barrier, inc=1, device_id=(fwd(k), g), device_id_type=MESH)
    for k in range(1, nz):
        pl.semaphore_signal(barrier, inc=1, device_id=zdev(lax.rem(zz + k, nz)), device_id_type=MESH)
    pl.semaphore_signal(barrier, inc=1, device_id=(b0, sib), device_id_type=MESH)
    loads[0].wait()
    pl.semaphore_wait(barrier, n + nz - 1)

    def bx(k):
        return copy(batch.at[mine], xall.at[b0, mine], bxs.at[k], bxr.at[k], (fwd(k), g))

    for k in range(1, n):
        bx(k).start()

    for load in loads[1:]:
        load.wait()
    eig_t = eigvec[...].T.astype(BF16)
    wv = weights[...]
    hi, lo = split(wv)
    w_hi[...] = hi
    w_lo[...] = lo
    cen_sq = jnp.sum(centers[...].astype(F32) ** 2, axis=1, keepdims=True)
    csq[...] = jnp.broadcast_to(cen_sq, (cen_sq.shape[0], rows)).T

    def fx(k):
        p = back(k)
        return copy(xall.at[p, mine], xall.at[p, mine], fxs.at[k], fxr.at[k], (b0, sib))

    def cp(k):
        p = back(k)
        return copy(pall.at[p, other], pc.at[p], cps.at[k], cpr.at[k], (b0, sib))

    def cm(k):
        p = back(k)
        return copy(mall.at[p, qother], mc.at[p], cms.at[k], cmr.at[k], (b0, sib))

    def bp(k, j):
        p, z = back(k), lax.rem(zz + j, nz)
        at = pl.ds(pl.multiple_of(c * half + rows_of(z), rz), rz)
        return copy(
            pall.at[p, at, cols_of(z)],
            pb.at[b0, pl.ds(rows_of(z), rz), cols_of(z)],
            bps.at[j * n + k], bpr.at[j * n + k], (p, g),
        )

    def bp_send(k):
        for j in list(range(1, nz)) + [0]:
            bp(k, j).start()
        bm(k).start()

    def bm(k):
        p = back(k)
        return copy(mall.at[p, qmine], mb.at[b0], bms.at[k], bmr.at[k], (p, g))

    def chunk(k, x):
        p = back(k)
        x_sq = jnp.sum(x.astype(F32) ** 2, axis=1, keepdims=True)
        dist = csq[...] + x_sq - 2.0 * dot_nt(x, centers[...])
        kt = jnp.exp(-dist * (4.0 / d))
        ktf[p] = kt
        khi, klo = split(kt)
        both = dot(jnp.concatenate([khi, klo], axis=0), w_hi[...])
        pall[p] = both[:rows] + both[rows:] + dot(khi, w_lo[...])
        mall[p] = dot_nt(eig_t, khi[:, :nys]).astype(BF16)
        cp(k).start()
        cm(k).start()

    def core_sum(k):
        p = back(k)
        cp(k).wait()
        cm(k).wait()
        pall[p, mine] = pall[p, mine] + pc[p]
        mall[p, qmine] = (mall[p, qmine].astype(F32) + mc[p].astype(F32)).astype(BF16)

    chunk(0, batch[...])

    def relay(k):
        bx(k).wait()
        fx(k).start()

    for k in range(1, min(3, n)):
        relay(k)

    def work(k, carry):
        fx(k).wait()
        chunk(k, xall[back(k)])

        @pl.when(k + 2 < n)
        def _():
            relay(k + 2)

        @pl.when(k >= 2)
        def _():
            core_sum(k - 1)
            bp_send(k - 1)

        return carry

    lax.fori_loop(1, n, work, 0)
    core_sum(n - 1)
    bp_send(n - 1)
    core_sum(0)

    def turn(p, carry):
        th, tl = split(ktf[p].T)
        at = pl.ds(pl.multiple_of(p * rows, rows), rows)
        k_hi[:, at] = th
        k_lo[:, at] = tl
        return carry

    lax.fori_loop(0, n // 4, turn, 0)

    def zp(k):
        z = lax.rem(zz + k, nz)
        return copy(
            acc.at[pl.ds(rows_of(z), rz), cols_of(z)], zb.at[zz], zps.at[k], zpr.at[k], zdev(z)
        )

    def zm(k):
        z = lax.rem(zz + k, nz)
        return copy(mz.at[zz], mz.at[zz], zms.at[k], zmr.at[k], zdev(z))

    def piece_sum(j):
        z = lax.rem(zz + j, nz)
        at = pl.ds(pl.multiple_of(c * half + rows_of(z), rz), rz)
        total = pall[b0, at, cols_of(z)]
        for k in range(1, n):
            bp(k, j).wait()
            total = total + pb[fwd(k), pl.ds(rows_of(z), rz), cols_of(z)]
        return total

    def piece_send(j, carry):
        z = lax.rem(zz + j, nz)
        acc[pl.ds(rows_of(z), rz), cols_of(z)] = piece_sum(j)
        zp(j).start()
        return carry

    lax.fori_loop(1, nz, piece_send, 0)
    total = piece_sum(0)
    macc[...] = mall[b0, qmine].astype(F32)
    for k in range(1, n):
        bm(k).wait()
        macc[...] += mb[fwd(k)].astype(F32)
    mz[zz] = macc[...].astype(BF16)
    lax.fori_loop(n // 4, n // 2, turn, 0)
    for k in range(1, nz):
        zp(k).wait()
        total = total + zb[lax.rem(zz + nz - k, nz)]
    my_rows = pl.ds(pl.multiple_of(c * half + rows_of(zz), rz), rz)
    my_cols = cols_of(zz)
    pred[my_rows, my_cols] = total
    rall[b0, my_rows, my_cols] = (total - targets[my_rows, my_cols]).astype(BF16)

    def gr(k):
        at = rall.at[b0, my_rows, my_cols]
        return copy(at, at, grs.at[k], grr.at[k], zdev(lax.rem(zz + k, nz)))

    def pr(k):
        at = pred.at[my_rows, my_cols]
        return copy(at, at, prs.at[k], prr.at[k], zdev(lax.rem(zz + k, nz)))

    for k in range(1, nz):
        gr(k).start()
    def gm(k):
        at = mfull.at[b0, qmine]
        return copy(at, at, gms.at[k], gmr.at[k], (fwd(k), g))

    def gb(k, j):
        z = lax.rem(zz + nz - j, nz)
        at = rall.at[
            b0, pl.ds(pl.multiple_of(c * half + rows_of(z), rz), rz), cols_of(z)
        ]
        return copy(at, at, gbs.at[j * n + k], gbr.at[j * n + k], (fwd(k), g))

    def gb_send(j, carry):
        gr(j).wait()
        for k in range(1, n):
            gb(k, j).start()
        return carry

    def fr(k):
        at = rall.at[back(k), mine]
        return copy(at, at, frs.at[k], frr.at[k], (b0, sib))

    def fm(k):
        at = mfull.at[back(k), qmine]
        return copy(at, at, fms.at[k], fmr.at[k], (b0, sib))

    for k in range(1, n):
        gb(k, 0).start()
    for k in range(1, nz):
        zm(k).start()
    lax.fori_loop(1, nz, gb_send, 0)
    fr(0).start()
    msum = mz[zz].astype(F32)
    for k in range(1, nz):
        zm(k).wait()
        msum = msum + mz[lax.rem(zz + nz - k, nz)].astype(F32)
    mfull[b0, qmine] = msum.astype(BF16)
    for k in range(1, n):
        gm(k).start()
    fm(0).start()
    for k in range(1, nz):
        pr(k).start()

    lax.fori_loop(n // 2, n, turn, 0)

    def gb_take(k, carry):
        for j in range(nz):
            gb(k, j).wait()
        fr(k).start()
        return carry

    lax.fori_loop(1, n, gb_take, 0)
    for k in range(1, n):
        gm(k).wait()
        fm(k).start()
    for k in range(1, nz):
        pr(k).wait()
    px = copy(pred.at[mine], pred.at[mine], pxs, pxr, (b0, sib))
    px.start()
    for k in range(n):
        fr(k).wait()

    res = rall[...].reshape(n * rows, outs)
    rate = step[0]
    tile = 256 if weights.shape[0] % 256 == 0 else nys

    def update(t, carry):
        at = pl.ds(pl.multiple_of(t * tile, tile), tile)
        grad = dot(k_hi[at, :], res) + dot(k_lo[at, :], res)
        new_out[at, :] = weights[at, :] - rate * grad
        return carry

    lax.fori_loop(0, weights.shape[0] // tile, update, 0)
    for k in range(n):
        fm(k).wait()
    proj = dot(mfull[0], rall[0])
    for p in range(1, n):
        proj = proj + dot(mfull[p], rall[p])
    corr = jnp.dot(
        eigvec[...] * eig_scale[...], proj, precision=lax.Precision.HIGHEST,
        preferred_element_type=F32,
    )
    new_out[:nys, :] = new_out[:nys, :] + rate * corr
    px.wait()
    pred_out[...] = pred[...]


def local(n, nz, batch, targets, centers, weights, eigvec, eig_scale, step):
    rows, d = batch.shape
    cen, outs = weights.shape
    q = eigvec.shape[1]
    half, qh = rows // 2, q // 2
    ncol = min(nz, outs // LANES)
    rz, cw = half // (nz // ncol), outs // ncol
    hbm = pl.BlockSpec(memory_space=pltpu.HBM)
    dma = pltpu.SemaphoreType.DMA
    return pl.pallas_call(
        functools.partial(kernel, n, nz),
        out_shape=(
            jax.ShapeDtypeStruct((rows, outs), F32),
            jax.ShapeDtypeStruct((cen, outs), F32),
        ),
        in_specs=[hbm] * 6 + [pl.BlockSpec(memory_space=pltpu.SMEM)],
        out_specs=(pl.BlockSpec(memory_space=pltpu.VMEM),) * 2,
        scratch_shapes=[
            pltpu.VMEM((rows, d), BF16),
            pltpu.VMEM((rows, outs), F32),
            pltpu.VMEM((cen, d), BF16),
            pltpu.VMEM((cen, outs), F32),
            pltpu.VMEM(eigvec.shape, F32),
            pltpu.VMEM((1, q), F32),
            pltpu.VMEM((n, rows, d), BF16),
            pltpu.VMEM((cen, outs), BF16),
            pltpu.VMEM((cen, outs), BF16),
            pltpu.VMEM((rows, cen), F32),
            pltpu.VMEM((n, rows, cen), F32),
            pltpu.VMEM((cen, n * rows), BF16),
            pltpu.VMEM((cen, n * rows), BF16),
            pltpu.VMEM((n, rows, outs), F32),
            pltpu.VMEM((n, q, rows), BF16),
            pltpu.VMEM((n, half, outs), F32),
            pltpu.VMEM((n, qh, rows), BF16),
            pltpu.VMEM((n, half, outs), F32),
            pltpu.VMEM((n, qh, rows), BF16),
            pltpu.VMEM((half, outs), F32),
            pltpu.VMEM((qh, rows), F32),
            pltpu.VMEM((nz, rz, cw), F32),
            pltpu.VMEM((nz, qh, rows), BF16),
            pltpu.VMEM((rows, outs), F32),
            pltpu.VMEM((n, rows, outs), BF16),
            pltpu.VMEM((n, q, rows), BF16),
        ]
        + [dma((n,))] * 8
        + [dma((n * nz,))] * 2
        + [dma((n,))] * 2
        + [dma((nz,))] * 6
        + [dma(()), dma(())]
        + [dma((nz,))] * 2
        + [dma((n * nz,))] * 2
        + [dma((n,))] * 6
        + [dma((6,))],
        compiler_params=pltpu.CompilerParams(
            collective_id=0, has_side_effects=True, vmem_limit_bytes=48 * 1024 * 1024
        ),
        cost_estimate=pl.CostEstimate(
            flops=10 * cen * n * rows * outs, bytes_accessed=12 * cen * outs,
            transcendentals=cen * n * rows,
        ),
    )(
        *(
            pltpu.with_memory_space_constraint(v, pltpu.HBM)
            for v in (batch, targets, centers, weights, eigvec, eig_scale[None, :])
        ),
        step,
    )


def solution(mesh):
    n, nz = mesh.shape["blk"], mesh.shape["grp"] // 2
    return jax.shard_map(
        functools.partial(local, n, nz),
        mesh=mesh,
        in_specs=(
            P("blk", None),
            P("blk", None),
            P(("blk", "grp"), None),
            P(("blk", "grp"), None),
            P(("blk", "grp"), None),
            P(),
            P(),
        ),
        out_specs=(P("blk", None), P(("blk", "grp"), None)),
        check_vma=False,
    )
```

```python
import functools

import jax
import jax.numpy as jnp
from jax import lax
from jax.experimental import pallas as pl
from jax.experimental.pallas import tpu as pltpu
from jax.sharding import PartitionSpec as P

MESH = pl.DeviceIdType.MESH
F32 = jnp.float32
BF16 = jnp.bfloat16
LANES = 128


def split(v):
    hi = v.astype(BF16)
    return hi, (v - hi.astype(F32)).astype(BF16)


def dot(a, b):
    return jnp.dot(a, b, preferred_element_type=F32)


def dot_nt(a, b):
    return lax.dot_general(a, b, (((1,), (1,)), ((), ())), preferred_element_type=F32)


def kernel(
    n, nz,
    batch_h, targets_h, centers_h, weights_h, eigvec_h, scale_h, step,
    pred_out, new_out,
    batch, targets, centers, weights, eigvec, eig_scale,
    xall, w_hi, w_lo, csq, ktf, k_hi, k_lo, pall, mall, pc, mc, pb, mb, acc, macc, zb, mz,
    pred, rall, mfull,
    bxs, bxr, fxs, fxr, cps, cpr, cms, cmr, bps, bpr, bms, bmr, zps, zpr, zms, zmr,
    prs, prr, pxs, pxr, grs, grr, gbs, gbr, gms, gmr, frs, frr, fms, fmr, ins,
):
    b0 = lax.axis_index("blk")
    g = lax.axis_index("grp")
    c = lax.rem(g, 2)
    zz = lax.div(g, 2)
    sib = g + 1 - 2 * c
    rows = batch.shape[0]
    half = rows // 2
    q = eigvec.shape[1]
    qh = q // 2
    nys = eigvec.shape[0]
    d = batch.shape[1]
    outs = weights.shape[1]
    ncol = min(nz, outs // LANES)
    cw = outs // ncol
    nrow = nz // ncol
    rz = half // nrow
    mine = pl.ds(pl.multiple_of(c * half, half), half)
    other = pl.ds(pl.multiple_of((1 - c) * half, half), half)
    qmine = pl.ds(pl.multiple_of(c * qh, qh), qh)
    qother = pl.ds(pl.multiple_of((1 - c) * qh, qh), qh)

    def copy(src, dst, ss, rs, to):
        return pltpu.make_async_remote_copy(
            src_ref=src, dst_ref=dst, send_sem=ss, recv_sem=rs, device_id=to, device_id_type=MESH
        )

    def fwd(k):
        peer, bit = 0, 1
        while bit < n:
            peer = peer + lax.rem(lax.div(b0, bit) + lax.div(jnp.int32(k), bit), 2) * bit
            bit *= 2
        return peer

    back = fwd

    def zdev(z):
        return (b0, z * 2 + c)

    loads = [
        pltpu.make_async_copy(src, dst, ins.at[i])
        for i, (src, dst) in enumerate(
            (
                (batch_h, batch),
                (centers_h, centers),
                (weights_h, weights),
                (eigvec_h, eigvec),
                (scale_h, eig_scale),
                (targets_h, targets),
            )
        )
    ]
    for load in loads:
        load.start()

    def rows_of(z):
        return pl.multiple_of(lax.div(z, ncol) * rz, rz)

    def cols_of(z):
        return pl.ds(pl.multiple_of(lax.rem(z, ncol) * cw, cw), cw)

    barrier = pltpu.get_barrier_semaphore()
    for k in range(1, n):
        pl.semaphore_signal(barrier, inc=1, device_id=(fwd(k), g), device_id_type=MESH)
    for k in range(1, nz):
        pl.semaphore_signal(barrier, inc=1, device_id=zdev(lax.rem(zz + k, nz)), device_id_type=MESH)
    pl.semaphore_signal(barrier, inc=1, device_id=(b0, sib), device_id_type=MESH)
    loads[0].wait()
    pl.semaphore_wait(barrier, n + nz - 1)

    def bx(k):
        return copy(batch.at[mine], xall.at[b0, mine], bxs.at[k], bxr.at[k], (fwd(k), g))

    for k in range(n - 1, 0, -1):
        bx(k).start()

    for load in loads[1:]:
        load.wait()
    eig_t = eigvec[...].T.astype(BF16)
    wv = weights[...]
    hi, lo = split(wv)
    w_hi[...] = hi
    w_lo[...] = lo
    cen_sq = jnp.sum(centers[...].astype(F32) ** 2, axis=1, keepdims=True)
    csq[...] = jnp.broadcast_to(cen_sq, (cen_sq.shape[0], rows)).T

    def fx(k):
        p = back(k)
        return copy(xall.at[p, mine], xall.at[p, mine], fxs.at[k], fxr.at[k], (b0, sib))

    def cp(k):
        p = back(k)
        return copy(pall.at[p, other], pc.at[p], cps.at[k], cpr.at[k], (b0, sib))

    def cm(k):
        p = back(k)
        return copy(mall.at[p, qother], mc.at[p], cms.at[k], cmr.at[k], (b0, sib))

    def bp(k, j):
        p, z = back(k), lax.rem(zz + j, nz)
        at = pl.ds(pl.multiple_of(c * half + rows_of(z), rz), rz)
        return copy(
            pall.at[p, at, cols_of(z)],
            pb.at[b0, pl.ds(rows_of(z), rz), cols_of(z)],
            bps.at[j * n + k], bpr.at[j * n + k], (p, g),
        )

    def bp_send(k):
        for j in list(range(1, nz)) + [0]:
            bp(k, j).start()
        bm(k).start()

    def bm(k):
        p = back(k)
        return copy(mall.at[p, qmine], mb.at[b0], bms.at[k], bmr.at[k], (p, g))

    def chunk(k, x):
        p = back(k)
        x_sq = jnp.sum(x.astype(F32) ** 2, axis=1, keepdims=True)
        dist = csq[...] + x_sq - 2.0 * dot_nt(x, centers[...])
        kt = jnp.exp(-dist * (4.0 / d))
        ktf[p] = kt
        khi, klo = split(kt)
        both = dot(jnp.concatenate([khi, klo], axis=0), w_hi[...])
        pall[p] = both[:rows] + both[rows:] + dot(khi, w_lo[...])
        mall[p] = dot_nt(eig_t, khi[:, :nys]).astype(BF16)
        cp(k).start()
        cm(k).start()

    def core_sum(k):
        p = back(k)
        cp(k).wait()
        cm(k).wait()
        pall[p, mine] = pall[p, mine] + pc[p]
        mall[p, qmine] = (mall[p, qmine].astype(F32) + mc[p].astype(F32)).astype(BF16)

    chunk(0, batch[...])

    def relay(k):
        bx(k).wait()
        fx(k).start()

    for k in range(1, min(3, n)):
        relay(k)

    def work(k, carry):
        fx(k).wait()
        chunk(k, xall[back(k)])

        @pl.when(k + 2 < n)
        def _():
            relay(k + 2)

        @pl.when(k >= 2)
        def _():
            core_sum(k - 1)
            bp_send(k - 1)

        return carry

    lax.fori_loop(1, n, work, 0)
    core_sum(n - 1)
    bp_send(n - 1)
    core_sum(0)

    def turn(p, carry):
        th, tl = split(ktf[p].T)
        at = pl.ds(pl.multiple_of(p * rows, rows), rows)
        k_hi[:, at] = th
        k_lo[:, at] = tl
        return carry

    lax.fori_loop(0, n // 4, turn, 0)

    def zp(k):
        z = lax.rem(zz + k, nz)
        return copy(
            acc.at[pl.ds(rows_of(z), rz), cols_of(z)], zb.at[zz], zps.at[k], zpr.at[k], zdev(z)
        )

    def zm(k):
        z = lax.rem(zz + k, nz)
        return copy(mz.at[zz], mz.at[zz], zms.at[k], zmr.at[k], zdev(z))

    def piece_sum(j):
        z = lax.rem(zz + j, nz)
        at = pl.ds(pl.multiple_of(c * half + rows_of(z), rz), rz)
        total = pall[b0, at, cols_of(z)]
        for k in range(1, n):
            bp(k, j).wait()
            total = total + pb[fwd(k), pl.ds(rows_of(z), rz), cols_of(z)]
        return total

    def piece_send(j, carry):
        z = lax.rem(zz + j, nz)
        acc[pl.ds(rows_of(z), rz), cols_of(z)] = piece_sum(j)
        zp(j).start()
        return carry

    lax.fori_loop(1, nz, piece_send, 0)
    total = piece_sum(0)
    macc[...] = mall[b0, qmine].astype(F32)
    for k in range(1, n):
        bm(k).wait()
        macc[...] += mb[fwd(k)].astype(F32)
    mz[zz] = macc[...].astype(BF16)
    lax.fori_loop(n // 4, n // 2, turn, 0)
    for k in range(1, nz):
        zp(k).wait()
        total = total + zb[lax.rem(zz + nz - k, nz)]
    my_rows = pl.ds(pl.multiple_of(c * half + rows_of(zz), rz), rz)
    my_cols = cols_of(zz)
    pred[my_rows, my_cols] = total
    rall[b0, my_rows, my_cols] = (total - targets[my_rows, my_cols]).astype(BF16)

    def gr(k):
        at = rall.at[b0, my_rows, my_cols]
        return copy(at, at, grs.at[k], grr.at[k], zdev(lax.rem(zz + k, nz)))

    def pr(k):
        at = pred.at[my_rows, my_cols]
        return copy(at, at, prs.at[k], prr.at[k], zdev(lax.rem(zz + k, nz)))

    for k in range(1, nz):
        gr(k).start()
    def gm(k):
        at = mfull.at[b0, qmine]
        return copy(at, at, gms.at[k], gmr.at[k], (fwd(k), g))

    def gb(k, j):
        z = lax.rem(zz + nz - j, nz)
        at = rall.at[
            b0, pl.ds(pl.multiple_of(c * half + rows_of(z), rz), rz), cols_of(z)
        ]
        return copy(at, at, gbs.at[j * n + k], gbr.at[j * n + k], (fwd(k), g))

    def gb_send(j, carry):
        gr(j).wait()
        for k in range(1, n):
            gb(k, j).start()
        return carry

    def fr(k):
        at = rall.at[back(k), mine]
        return copy(at, at, frs.at[k], frr.at[k], (b0, sib))

    def fm(k):
        at = mfull.at[back(k), qmine]
        return copy(at, at, fms.at[k], fmr.at[k], (b0, sib))

    for k in range(1, n):
        gb(k, 0).start()
    for k in range(1, nz):
        zm(k).start()
    lax.fori_loop(1, nz, gb_send, 0)
    fr(0).start()
    msum = mz[zz].astype(F32)
    for k in range(1, nz):
        zm(k).wait()
        msum = msum + mz[lax.rem(zz + nz - k, nz)].astype(F32)
    mfull[b0, qmine] = msum.astype(BF16)
    for k in range(1, n):
        gm(k).start()
    fm(0).start()
    for k in range(1, nz):
        pr(k).start()

    lax.fori_loop(n // 2, n, turn, 0)

    def gb_take(k, carry):
        for j in range(nz):
            gb(k, j).wait()
        fr(k).start()
        return carry

    lax.fori_loop(1, n, gb_take, 0)
    for k in range(1, n):
        gm(k).wait()
        fm(k).start()
    for k in range(1, nz):
        pr(k).wait()
    px = copy(pred.at[mine], pred.at[mine], pxs, pxr, (b0, sib))
    px.start()
    for k in range(n):
        fr(k).wait()

    res = rall[...].reshape(n * rows, outs)
    rate = step[0]
    tile = 256 if weights.shape[0] % 256 == 0 else nys

    def update(t, carry):
        at = pl.ds(pl.multiple_of(t * tile, tile), tile)
        grad = dot(k_hi[at, :], res) + dot(k_lo[at, :], res)
        new_out[at, :] = weights[at, :] - rate * grad
        return carry

    lax.fori_loop(0, weights.shape[0] // tile, update, 0)
    for k in range(n):
        fm(k).wait()
    proj = dot(mfull[0], rall[0])
    for p in range(1, n):
        proj = proj + dot(mfull[p], rall[p])
    corr = jnp.dot(
        eigvec[...] * eig_scale[...], proj, precision=lax.Precision.HIGHEST,
        preferred_element_type=F32,
    )
    new_out[:nys, :] = new_out[:nys, :] + rate * corr
    px.wait()
    pred_out[...] = pred[...]


def local(n, nz, batch, targets, centers, weights, eigvec, eig_scale, step):
    rows, d = batch.shape
    cen, outs = weights.shape
    q = eigvec.shape[1]
    half, qh = rows // 2, q // 2
    ncol = min(nz, outs // LANES)
    rz, cw = half // (nz // ncol), outs // ncol
    hbm = pl.BlockSpec(memory_space=pltpu.HBM)
    dma = pltpu.SemaphoreType.DMA
    return pl.pallas_call(
        functools.partial(kernel, n, nz),
        out_shape=(
            jax.ShapeDtypeStruct((rows, outs), F32),
            jax.ShapeDtypeStruct((cen, outs), F32),
        ),
        in_specs=[hbm] * 6 + [pl.BlockSpec(memory_space=pltpu.SMEM)],
        out_specs=(pl.BlockSpec(memory_space=pltpu.VMEM),) * 2,
        scratch_shapes=[
            pltpu.VMEM((rows, d), BF16),
            pltpu.VMEM((rows, outs), F32),
            pltpu.VMEM((cen, d), BF16),
            pltpu.VMEM((cen, outs), F32),
            pltpu.VMEM(eigvec.shape, F32),
            pltpu.VMEM((1, q), F32),
            pltpu.VMEM((n, rows, d), BF16),
            pltpu.VMEM((cen, outs), BF16),
            pltpu.VMEM((cen, outs), BF16),
            pltpu.VMEM((rows, cen), F32),
            pltpu.VMEM((n, rows, cen), F32),
            pltpu.VMEM((cen, n * rows), BF16),
            pltpu.VMEM((cen, n * rows), BF16),
            pltpu.VMEM((n, rows, outs), F32),
            pltpu.VMEM((n, q, rows), BF16),
            pltpu.VMEM((n, half, outs), F32),
            pltpu.VMEM((n, qh, rows), BF16),
            pltpu.VMEM((n, half, outs), F32),
            pltpu.VMEM((n, qh, rows), BF16),
            pltpu.VMEM((half, outs), F32),
            pltpu.VMEM((qh, rows), F32),
            pltpu.VMEM((nz, rz, cw), F32),
            pltpu.VMEM((nz, qh, rows), BF16),
            pltpu.VMEM((rows, outs), F32),
            pltpu.VMEM((n, rows, outs), BF16),
            pltpu.VMEM((n, q, rows), BF16),
        ]
        + [dma((n,))] * 8
        + [dma((n * nz,))] * 2
        + [dma((n,))] * 2
        + [dma((nz,))] * 6
        + [dma(()), dma(())]
        + [dma((nz,))] * 2
        + [dma((n * nz,))] * 2
        + [dma((n,))] * 6
        + [dma((6,))],
        compiler_params=pltpu.CompilerParams(
            collective_id=0, has_side_effects=True, vmem_limit_bytes=48 * 1024 * 1024
        ),
        cost_estimate=pl.CostEstimate(
            flops=10 * cen * n * rows * outs, bytes_accessed=12 * cen * outs,
            transcendentals=cen * n * rows,
        ),
    )(
        *(
            pltpu.with_memory_space_constraint(v, pltpu.HBM)
            for v in (batch, targets, centers, weights, eigvec, eig_scale[None, :])
        ),
        step,
    )


def solution(mesh):
    n, nz = mesh.shape["blk"], mesh.shape["grp"] // 2
    return jax.shard_map(
        functools.partial(local, n, nz),
        mesh=mesh,
        in_specs=(
            P("blk", None),
            P("blk", None),
            P(("blk", "grp"), None),
            P(("blk", "grp"), None),
            P(("blk", "grp"), None),
            P(),
            P(),
        ),
        out_specs=(P("blk", None), P(("blk", "grp"), None)),
        check_vma=False,
    )
```
